768 devices in a mesh: dp: 48 (over z, x), expert: 16 (over y, core).
Axes of the slice: x: 4, y: 8, z: 12, core: 2. Of those that a mesh axis runs over, the one named last changes fastest.
Arguments:
- tokens: bfloat16 [98304, 4096], P(('dp', 'expert')), may hold values from -6 to 6
- routes: int32 [98304, 2], P(('dp', 'expert')), may hold values from 0 to 7, all different within a row; in each aligned block of 128 rows (0 to 127, 128 to 255, ...) at most 32 rows name the same one
- route_weights: float32 [98304, 2], P(('dp', 'expert')), may hold values from 0.3 to 1.5
- w_gate: bfloat16 [16, 4096, 256], P('expert'), may hold values from -0.09375 to 0.09375
- w_up: bfloat16 [16, 4096, 256], P('expert'), may hold values from -0.09375 to 0.09375
- w_down: bfloat16 [16, 256, 4096], P('expert'), may hold values from -0.375 to 0.375
- rms_gain: float32 [4096], replicated, may hold values from 0.5 to 1.5
- query_len: int32 [768], P(('dp', 'expert')), may hold values from 1 to 32
- passage_len: int32 [768], P(('dp', 'expert')), may hold values from 1 to 96
- positive: int32 [16, 48], P('expert', 'dp'), may hold values from 0 to 47, each once within a row
- logit_scale: float32 [16, 48], P('expert', 'dp'), may hold values from 10 to 300
Outputs:
- layer_out: bfloat16 [98304, 4096], P(('dp', 'expert'))
- embed_grads: float32 [768, 2, 4096], P(('dp', 'expert'))
The draws below stay inside these ranges and needn't reach their ends.
Inputs may be any that keep to these rules, and one draw needn't show every extreme that they name: `routes`: in each device's 128 rows every expert is named by exactly 32 rows, and the two experts of a row differ. `positive`: for each expert index the positives are a permutation of the dp indices.
All inputs are finite; a program needn't handle non-finite values.
Results may differ from the reference program's by a relative error of at most 0.034.
Values may be sent and summed in bfloat16 or wider, within the bound.
A program may use at most 64 MiB of HBM per device.

```python
import math
import jax
import jax.numpy as jnp
import numpy as np
from jax import lax

D = 4096
FF_DEV = 256
TOK_DEV = 128
EXPERTS = 8
TOKENS = 98304
QLEN = 32
PLEN = 96
CAP = 32
N_DP = 48
N_EXPERT = 16
DEVICES = 768


def draw_tokens(key, part):
    key = jax.random.fold_in(key, 1)
    noise_key = jax.random.fold_in(key, 0)
    fresh_noise = jnp.clip(jax.random.normal(noise_key, (TOKENS, D), jnp.float32), -6.0, 6.0)
    return fresh_noise.astype(jnp.bfloat16)


def touch_ends(values, rng, smallest, top_value):
    longest = values.shape.index(max(values.shape))
    spots = []
    for shift in (0, 1):
        where = [jax.random.randint(jax.random.fold_in(rng, axis), (), 0, length) for axis, length in enumerate(values.shape)]
        where[longest] = (where[longest] + shift) % values.shape[longest]
        spots.append(tuple(where))
    return values.at[spots[0]].set(smallest).at[spots[1]].set(top_value)


def steps_of(key, extent, cuts, smallest, high):
    def one(dim, parts):
        heights = jax.random.uniform(jax.random.fold_in(jax.random.fold_in(key, 6), dim), (parts,), jnp.float32, smallest / len(cuts), high / len(cuts))
        return jnp.repeat(jnp.exp(heights), extent[dim] // parts).reshape((-1,) + (1,) * (len(extent) - dim - 1))

    factor_of = one(*cuts[0])
    for cut in cuts[1:]:
        factor_of = factor_of * one(*cut)
    return factor_of


def routed_block(rng, own, number, rows, count, top, bound, lean):
    ranking = jax.random.permutation(rng, count)
    heavy_load, usual = load_shares(count, rows * top, bound, lean, True), load_shares(count, rows * top, bound, lean, False)
    places = jnp.arange(count)

    def named(lengths, turn):
        used = int((lengths > 0).sum())
        fixed = max(1, used // 4)
        shifted = fixed + (places - fixed + turn * (used - fixed)) % max(1, count - fixed)
        return jnp.zeros((count,), jnp.int32).at[ranking[jnp.where(places < fixed, places, shifted)]].set(jnp.asarray(lengths, jnp.int32))

    lengths = jnp.where(number % 4 == 0, named(heavy_load, number // 4), named(usual, number - number // 4 - 1))
    mixed = jax.random.permutation(jax.random.fold_in(own, 3), count)
    source_of, sink = mixed[0:count // 2 * 2:2], mixed[1:count // 2 * 2:2]
    room = jnp.minimum(lengths[source_of] - 1, bound - lengths[sink]) // 2
    room = jnp.where((source_of == ranking[0]) | (sink == ranking[0]) | (lengths[sink] == 0), 0, jnp.maximum(room, 0))
    shifted = jax.random.randint(jax.random.fold_in(own, 4), (count // 2,), 0, 1 << 20) % (room + 1)
    lengths = lengths.at[source_of].add(-shifted).at[sink].add(shifted)
    labels = jnp.searchsorted(jnp.cumsum(lengths), jnp.arange(rows * top), side="right").astype(jnp.int32)
    listing = labels.reshape(top, rows).T
    listing = listing[jax.random.permutation(jax.random.fold_in(own, 1), rows)]
    turn = jax.random.randint(jax.random.fold_in(own, 2), (rows, 1), 0, top)
    return jnp.take_along_axis(listing, (jnp.arange(top)[None, :] + turn) % top, axis=1)


def load_shares(number_of, total, bound, lean, full):
    weights = [(1 << 20) // math.isqrt(standing ** lean) + 1 for standing in range(1, number_of + 1)]
    largest = bound if full else min(bound, max(-(-total // number_of), total * weights[0] // sum(weights)))
    least = 1 if total - largest >= number_of - 1 else 0
    given, rest = [largest] + [least] * (number_of - 1), total - largest - least * (number_of - 1)
    while rest > 0:
        free = [i for i in range(1, number_of) if given[i] < largest] or [i for i in range(1, number_of) if given[i] < bound]
        mass, remaining = sum([weights[i] for i in free]), rest
        for i in free:
            more = min(bound - given[i], max(1, remaining * weights[i] // mass), rest)
            given[i] = given[i] + more
            rest = rest - more
    return np.array(given)


def noise(stream_key, shape, width, reach, shards=(), kind=jnp.bfloat16):
    values = width * jax.random.normal(stream_key, shape, jnp.float32)
    if shards:
        values = values * steps_of(stream_key, shape, shards, -0.22, 0.18)
    return jnp.clip(values, -reach, reach).astype(kind)


def setup_inputs(seed: int = 0) -> dict:
    key_list = jax.random.split(jax.random.key(seed), 12)
    tokens = draw_tokens(jax.random.fold_in(key_list[11], 71), 0)
    routes_keys = jax.random.split(jax.random.fold_in(key_list[1], 1), TOKENS // TOK_DEV)
    routes_turns = jax.random.permutation(jax.random.fold_in(key_list[1], 3), TOKENS // TOK_DEV)
    routes = jax.vmap(lambda own, number: routed_block(jax.random.fold_in(key_list[1], 2), own, number, TOK_DEV, EXPERTS, 2, CAP, 2))(routes_keys, routes_turns).reshape((TOKENS, 2))
    route_weights = jnp.clip(jnp.exp(math.log(1.5) - 1.60943787 * jax.random.uniform(key_list[2], (TOKENS, 2), jnp.float32) ** steps_of(key_list[2], (TOKENS, 2), ((0, 768),), -0.2, 0.2)), 0.3, 1.5)
    w_gate = noise(key_list[3], (N_EXPERT, D, FF_DEV), D ** -0.5, 0.09375, ((0, 16),))
    w_up = noise(key_list[4], (N_EXPERT, D, FF_DEV), D ** -0.5, 0.09375, ((0, 16),))
    w_down = noise(key_list[5], (N_EXPERT, FF_DEV, D), FF_DEV ** -0.5, 0.375, ((0, 16),))
    rms_gain = jnp.clip(1.0 + 0.1 * jax.random.normal(key_list[6], (D,), jnp.float32), 0.5, 1.5)
    query_len = touch_ends(jax.random.randint(key_list[7], (DEVICES,), 1, QLEN + 1), jax.random.fold_in(key_list[7], 1), 1, QLEN).astype(jnp.int32)
    passage_len = touch_ends(jax.random.randint(key_list[8], (DEVICES,), 1, PLEN + 1), jax.random.fold_in(key_list[8], 1), 1, PLEN).astype(jnp.int32)
    positive = jax.vmap(lambda own: jax.random.permutation(own, N_DP))(jax.random.split(key_list[9], N_EXPERT)).reshape((N_EXPERT, N_DP)).astype(jnp.int32)
    logit_scale = jnp.clip(jnp.exp(math.log(300.0) - 3.4011974 * jax.random.uniform(key_list[10], (N_EXPERT, N_DP), jnp.float32) ** steps_of(key_list[10], (N_EXPERT, N_DP), ((0, 16), (1, 48)), -0.2, 0.2)), 10.0, 300.0)
    return {"tokens": tokens, "routes": routes, "route_weights": route_weights, "w_gate": w_gate, "w_up": w_up, "w_down": w_down, "rms_gain": rms_gain, "query_len": query_len, "passage_len": passage_len, "positive": positive, "logit_scale": logit_scale}


highest = lax.Precision.HIGHEST

def slot_targets(route_block, expert_count, cap_slots):
    flat_routes = route_block.reshape(-1)
    one_hot = (flat_routes[:, None] == jnp.arange(expert_count, dtype=jnp.int32)[None, :]).astype(jnp.int32)
    running = jnp.cumsum(one_hot, axis=0) - 1
    return (flat_routes * cap_slots + lax.optimization_barrier(jnp.sum(one_hot * running, axis=1))).astype(jnp.int32)

def through_bfloat(values):
    return lax.optimization_barrier(values.astype(jnp.bfloat16)).astype(jnp.float32)

def unit_vector(vector):
    return vector * lax.rsqrt(jnp.sum(vector * vector) + 1e-06)

def pooled_pair(layer_block, gain, query_count, passage_count, query_slots):
    lifted = layer_block.astype(jnp.float32)
    normed = lifted * lax.rsqrt(lax.optimization_barrier(jnp.mean(lifted * lifted, axis=-1, keepdims=True)) + 1e-05) * gain
    position = jnp.arange(layer_block.shape[0], dtype=jnp.int32)
    query_mask = (position < query_count).astype(jnp.float32)
    passage_mask = ((position >= query_slots) & (position < query_slots + passage_count)).astype(jnp.float32)
    query_vec = jnp.dot(query_mask, normed, precision=highest) / query_count.astype(jnp.float32)
    passage_vec = jnp.dot(passage_mask, normed, precision=highest) / passage_count.astype(jnp.float32)
    return (unit_vector(query_vec), unit_vector(passage_vec))

def reference(tokens, routes, route_weights, w_gate, w_up, w_down, rms_gain, query_len, passage_len, positive, logit_scale):
    gate_all = w_gate.astype(jnp.float32).reshape(EXPERTS, 2, D, FF_DEV)
    up_all = w_up.astype(jnp.float32).reshape(EXPERTS, 2, D, FF_DEV)
    down_all = w_down.astype(jnp.float32).reshape(EXPERTS, 2, FF_DEV, D)
    token_blocks = tokens.reshape(DEVICES, TOK_DEV, D)
    route_blocks = routes.reshape(DEVICES, TOK_DEV, 2)
    weight_blocks = route_weights.reshape(DEVICES, TOK_DEV, 2)

    def one_block(inputs):
        token_block, route_block, weight_block, query_count, passage_count = inputs
        targets = slot_targets(route_block, EXPERTS, CAP)
        buffer = jnp.zeros((EXPERTS * CAP, D), jnp.bfloat16).at[targets].set(jnp.repeat(token_block, 2, axis=0))
        expert_rows = buffer.reshape(EXPERTS, CAP, D).astype(jnp.float32)
        gate_proj = jnp.einsum('ecd,ehdf->ehcf', expert_rows, gate_all, precision=highest)
        up_proj = jnp.einsum('ecd,ehdf->ehcf', expert_rows, up_all, precision=highest)
        hidden = through_bfloat(jax.nn.silu(gate_proj) * up_proj)
        partial_value = through_bfloat(jnp.einsum('ehcf,ehfd->ehcd', hidden, down_all, precision=highest))
        combined = (partial_value[:, 0] + partial_value[:, 1]).astype(jnp.bfloat16).reshape(EXPERTS * CAP, D)
        outputs = combined[targets].astype(jnp.float32).reshape(TOK_DEV, 2, D)
        layer_block = (token_block.astype(jnp.float32) + lax.optimization_barrier(jnp.sum(weight_block[:, :, None] * outputs, axis=1))).astype(jnp.bfloat16)
        query_unit, passage_unit = pooled_pair(layer_block, rms_gain, query_count, passage_count, QLEN)
        return (layer_block, query_unit, passage_unit)
    layer, query_units, passage_units = lax.map(one_block, (token_blocks, route_blocks, weight_blocks, query_len, passage_len))
    queries = query_units.reshape(N_DP, N_EXPERT, D).transpose(1, 0, 2)
    passages = passage_units.reshape(N_DP, N_EXPERT, D).transpose(1, 0, 2)
    scores = logit_scale[:, :, None] * jnp.einsum('jid,jmd->jim', queries, passages, precision=highest)
    largest = lax.optimization_barrier(jnp.max(scores, axis=-1, keepdims=True))
    expos = jnp.exp(scores - largest)
    probs = expos / lax.optimization_barrier(jnp.sum(expos, axis=-1, keepdims=True))
    target_rows = (positive[:, :, None] == jnp.arange(N_DP, dtype=jnp.int32)[None, None, :]).astype(jnp.float32)
    coefficient = (probs - target_rows) * logit_scale[:, :, None] / N_DP
    query_grad = jnp.einsum('jim,jmd->jid', coefficient, passages, precision=highest)
    passage_grad = jnp.einsum('jim,jid->jmd', coefficient, queries, precision=highest)
    grads = jnp.stack([query_grad, passage_grad], axis=2).transpose(1, 0, 2, 3).reshape(DEVICES, 2, D)
    return (layer.reshape(TOKENS, D), grads)
```

```python
import functools

import jax
import jax.numpy as jnp
from jax import lax
from jax.experimental import pallas as pl
from jax.experimental.pallas import tpu as pltpu
from jax.sharding import PartitionSpec as P

MESH = pl.DeviceIdType.MESH
HIGHEST = lax.Precision.HIGHEST
F32 = jnp.float32
BF16 = jnp.bfloat16

PLANES = 8
ZS = 12
XS = 4
CAP = 32
HALF = 16
TOK = 128
D = 4096
FF = 256
QLEN = 32
META = 128
WIDE = D + META
CHUNK = WIDE // 3
RANKS = 2 * ZS * XS

OFFSET = (0, 1, 7, 2, 6, 3, 5, 4)
OPPOSITE = (0, 2, 1, 4, 3, 6, 5, 7)
SEND_ORDER = (7, 5, 6, 3, 4, 1, 2, 0)
GROUPS = ((5, 8), (3, 5), (0, 3))


def moe_kernel(
    tok_ref,
    routes_ref,
    rw_ref,
    gain_ref,
    lens_ref,
    wg_ref,
    wu_ref,
    wd_ref,
    layer_ref,
    unit_ref,
    sbuf,
    rbuf,
    obuf,
    ret,
    wgv,
    wuv,
    wdv,
    vec,
    copy_sem,
    wsend_sem,
    wrecv_sem,
    dsend_sem,
    drecv_sem,
    csend_sem,
    crecv_sem,
):
    dp = lax.axis_index("dp")
    ex = lax.axis_index("expert")
    plane, core = ex // 2, lax.rem(ex, 2)

    def peer(offset, its_core):
        return (dp, lax.rem(plane + offset, PLANES) * 2 + its_core)

    barrier = pltpu.get_barrier_semaphore()
    for offset in range(PLANES):
        for flip in range(2):
            if offset or flip:
                pl.semaphore_signal(
                    barrier, inc=1, device_id=peer(offset, lax.rem(core + flip, 2)), device_id_type=MESH
                )

    pairs = ((wg_ref, wgv), (wu_ref, wuv), (wd_ref, wdv))
    own_weights = [
        pltpu.make_async_copy(src.at[0], dst.at[core], copy_sem.at[i])
        for i, (src, dst) in enumerate(pairs)
    ]
    for copy in own_weights:
        copy.start()

    route0 = routes_ref[0:1, :]
    route1 = routes_ref[1:2, :]
    experts = lax.broadcasted_iota(jnp.int32, (8, TOK), 0)
    named = ((route0 == experts) | (route1 == experts)).astype(F32)
    earlier = (
        lax.broadcasted_iota(jnp.int32, (TOK, TOK), 0) < lax.broadcasted_iota(jnp.int32, (TOK, TOK), 1)
    ).astype(BF16)
    slot = jnp.dot(named.astype(BF16), earlier, preferred_element_type=F32)
    row = lax.broadcasted_iota(jnp.int32, (PLANES * CAP, 1), 0)
    place = row // CAP
    offset_of = jnp.where(place % 2 == 1, (place + 1) // 2, (PLANES - place // 2) % PLANES)
    expert_of = (plane + offset_of) % PLANES
    spread = (expert_of == lax.broadcasted_iota(jnp.int32, (PLANES * CAP, 8), 1)).astype(BF16)
    slot_of = jnp.dot(spread, slot.astype(BF16), preferred_element_type=F32)
    fits = slot_of == (row % CAP).astype(F32)
    hot0 = (fits & (route0 == expert_of)).astype(F32)
    hot1 = (fits & (route1 == expert_of)).astype(F32)
    hot = (hot0 + hot1).astype(BF16)
    blend = (hot0 * rw_ref[0:1, :] + hot1 * rw_ref[1:2, :]).T
    blend_high = blend.astype(BF16)
    blend_low = (blend - blend_high.astype(F32)).astype(BF16)

    pl.semaphore_wait(barrier, 2 * PLANES - 1)

    swaps = [
        pltpu.make_async_remote_copy(
            src.at[0],
            dst.at[core],
            wsend_sem.at[i],
            wrecv_sem.at[i],
            device_id=peer(0, 1 - core),
            device_id_type=MESH,
        )
        for i, (src, dst) in enumerate(pairs)
    ]
    for copy in swaps:
        copy.start()

    def dispatch(p, half):
        return pltpu.make_async_remote_copy(
            sbuf.at[2 * p + half],
            rbuf.at[2 * OPPOSITE[p] + core],
            dsend_sem.at[2 * p + half],
            drecv_sem.at[2 * OPPOSITE[p] + core],
            device_id=peer(OFFSET[p], half),
            device_id_type=MESH,
        )

    for p in SEND_ORDER:
        rows = jnp.dot(hot[p * CAP : (p + 1) * CAP], tok_ref[...], preferred_element_type=F32).astype(BF16)
        sbuf[2 * p : 2 * p + 2] = rows.reshape(2, HALF, D)
        if p:
            for half in range(2):
                dispatch(p, half).start()
    keep = pltpu.make_async_copy(sbuf.at[core], rbuf.at[core], copy_sem.at[3])
    keep.start()
    give = pltpu.make_async_remote_copy(
        sbuf.at[1 - core],
        rbuf.at[core],
        dsend_sem.at[0],
        drecv_sem.at[0],
        device_id=peer(0, 1 - core),
        device_id_type=MESH,
    )
    give.start()

    for copy in own_weights:
        copy.wait()
    for copy in swaps:
        copy.wait()

    def give_back(q, half):
        return pltpu.make_async_remote_copy(
            obuf.at[2 * q + half],
            ret.at[2 * OPPOSITE[q] + core],
            csend_sem.at[2 * q + half],
            crecv_sem.at[2 * OPPOSITE[q] + core],
            device_id=peer(OFFSET[q], half),
            device_id_type=MESH,
        )

    for low, high in GROUPS:
        count = (high - low) * CAP
        for q in range(low, high):
            if q:
                for half in range(2):
                    pltpu.make_async_copy(
                        rbuf.at[2 * q + half], rbuf.at[2 * q + half], drecv_sem.at[2 * q + half]
                    ).wait()
            else:
                keep.wait()
                give.wait()
        hidden = []
        for h in range(2):
            gate = jnp.dot(
                rbuf[2 * low : 2 * high].reshape(count, D), wgv[h], preferred_element_type=F32
            )
            up = jnp.dot(rbuf[2 * low : 2 * high].reshape(count, D), wuv[h], preferred_element_type=F32)
            hidden.append((gate / (1.0 + jnp.exp(-gate)) * up).astype(BF16))
        for t in range(4):
            cols = slice(t * 1024, (t + 1) * 1024)
            part0 = jnp.dot(hidden[0], wdv[0, :, cols], preferred_element_type=F32).astype(BF16)
            part1 = jnp.dot(hidden[1], wdv[1, :, cols], preferred_element_type=F32).astype(BF16)
            total = (part0.astype(F32) + part1.astype(F32)).astype(BF16)
            obuf[2 * low : 2 * high, :, cols] = total.reshape(2 * (high - low), HALF, 1024)
        for q in reversed(range(low, high)):
            if q:
                for half in range(2):
                    give_back(q, half).start()
    keep = pltpu.make_async_copy(obuf.at[core], ret.at[core], copy_sem.at[3])
    keep.start()
    give = pltpu.make_async_remote_copy(
        obuf.at[1 - core],
        ret.at[core],
        csend_sem.at[0],
        crecv_sem.at[0],
        device_id=peer(0, 1 - core),
        device_id_type=MESH,
    )
    give.start()

    for p in range(1, PLANES):
        for half in range(2):
            dispatch(p, half).wait_send()
            give_back(p, half).wait_send()
    keep.wait()
    give.wait()
    for i in range(2, 2 * PLANES):
        pltpu.make_async_copy(ret.at[i], ret.at[i], crecv_sem.at[i]).wait()

    squares = jnp.zeros((TOK, 1), F32)
    for t in range(8):
        cols = slice(t * 512, (t + 1) * 512)
        outs = ret[:, :, cols].reshape(PLANES * CAP, 512)
        mixed = jnp.dot(blend_high, outs, preferred_element_type=F32) + jnp.dot(
            blend_low, outs, preferred_element_type=F32
        )
        block = (tok_ref[:, cols].astype(F32) + mixed).astype(BF16)
        layer_ref[:, cols] = block
        lifted = block.astype(F32)
        squares += jnp.sum(lifted * lifted, axis=1, keepdims=True)
    scale = lax.rsqrt(squares / D + 1e-05)
    position = lax.broadcasted_iota(jnp.int32, (TOK, 1), 0)
    q_len, p_len = lens_ref[0], lens_ref[1]
    q_coef = jnp.where(position < q_len, scale, 0.0) / q_len.astype(F32)
    p_coef = jnp.where((position >= QLEN) & (position < QLEN + p_len), scale, 0.0) / p_len.astype(F32)
    q_sum = jnp.zeros((1, 1), F32)
    p_sum = jnp.zeros((1, 1), F32)
    for t in range(8):
        cols = slice(t * 512, (t + 1) * 512)
        lifted = layer_ref[:, cols].astype(F32)
        gain = gain_ref[:, cols]
        q_vec = jnp.sum(lifted[:QLEN] * q_coef[:QLEN], axis=0, keepdims=True) * gain
        p_vec = jnp.sum(lifted[QLEN:] * p_coef[QLEN:], axis=0, keepdims=True) * gain
        q_sum += jnp.sum(q_vec * q_vec, axis=1, keepdims=True)
        p_sum += jnp.sum(p_vec * p_vec, axis=1, keepdims=True)
        vec[0:1, cols] = q_vec
        vec[1:2, cols] = p_vec
    unit_ref[0:1, :] = vec[0:1, :] * lax.rsqrt(q_sum + 1e-06)
    unit_ref[1:2, :] = vec[1:2, :] * lax.rsqrt(p_sum + 1e-06)


def loss_kernel(
    unit_ref, positive_ref, sharp_ref, grads_ref, line, units, xsend_sem, xrecv_sem, zsend_sem, zrecv_sem
):
    dp = lax.axis_index("dp")
    ex = lax.axis_index("expert")
    z, x = dp // XS, lax.rem(dp, XS)

    def along_x(step):
        return (z * XS + lax.rem(x + step, XS), ex)

    def along_z(step):
        return (lax.rem(z + step + ZS, ZS) * XS + x, ex)

    barrier = pltpu.get_barrier_semaphore()
    for step in range(1, XS):
        pl.semaphore_signal(barrier, inc=1, device_id=along_x(step), device_id_type=MESH)
    for step in (-1, 1):
        pl.semaphore_signal(barrier, inc=1, device_id=along_z(step), device_id_type=MESH)

    lane = lax.broadcasted_iota(jnp.int32, (2, META), 1)
    line[x, :, 0:D] = unit_ref[...]
    line[x, :, D:WIDE] = jnp.where(
        lane == 0, sharp_ref[0, 0], jnp.where(lane == 1, positive_ref[0, 0].astype(F32), 0.0)
    )
    pl.semaphore_wait(barrier, XS + 1)
    sends = [
        pltpu.make_async_remote_copy(
            line.at[x],
            line.at[x],
            xsend_sem.at[step],
            xrecv_sem.at[x],
            device_id=along_x(step),
            device_id_type=MESH,
        )
        for step in range(1, XS)
    ]
    for copy in sends:
        copy.start()
    for step in range(1, XS):
        source = lax.rem(x + step, XS)
        pltpu.make_async_copy(line.at[source], line.at[source], xrecv_sem.at[source]).wait()
    for i in range(XS):
        units[z, 2 * i : 2 * i + 2, :] = line[i]

    def hop(step, side, part):
        block = lax.rem(z - side * step + 2 * ZS, ZS)
        cols = pl.ds(part * CHUNK, CHUNK)
        return pltpu.make_async_remote_copy(
            units.at[block, :, cols],
            units.at[block, :, cols],
            zsend_sem.at[step, (side + 1) // 2, part],
            zrecv_sem.at[block, part],
            device_id=along_z(side),
            device_id_type=MESH,
        )

    def arrived(step, side, part):
        block = lax.rem(z - side * step + 2 * ZS, ZS)
        cols = pl.ds(part * CHUNK, CHUNK)
        pltpu.make_async_copy(
            units.at[block, :, cols], units.at[block, :, cols], zrecv_sem.at[block, part]
        ).wait()

    hops = ZS // 2
    for step in range(hops):
        for part in range(3):
            for side in (1, -1):
                if step:
                    arrived(step, side, part)
                if side == 1 or step < hops - 1:
                    hop(step, side, part).start()
    for part in range(3):
        arrived(hops, 1, part)
    for copy in sends:
        copy.wait_send()
    for step in range(hops):
        for part in range(3):
            for side in (1, -1):
                if side == 1 or step < hops - 1:
                    hop(step, side, part).wait_send()

    every = units[:, :, 0:D].reshape(RANKS, D)
    meta = units[:, :, D:WIDE].reshape(RANKS, META)
    sharp, positive = meta[:, 0:1], meta[:, 1:2]
    gram = lax.dot_general(
        every, every, (((1,), (1,)), ((), ())), precision=HIGHEST, preferred_element_type=F32
    )
    row = lax.broadcasted_iota(jnp.int32, (RANKS, RANKS), 0)
    col = lax.broadcasted_iota(jnp.int32, (RANKS, RANKS), 1)
    is_passage = col % 2 == 1
    scores = jnp.where(is_passage, gram * sharp, -jnp.inf)
    expos = jnp.exp(scores - jnp.max(scores, axis=1, keepdims=True))
    probs = expos / jnp.sum(expos, axis=1, keepdims=True)
    target = (is_passage & ((col // 2).astype(F32) == positive)).astype(F32)
    coef = jnp.where((row % 2 == 0) & is_passage, (probs - target) * sharp / (RANKS // 2), 0.0)
    pick_row = lax.broadcasted_iota(jnp.int32, (8, RANKS), 0)
    pick_col = lax.broadcasted_iota(jnp.int32, (8, RANKS), 1)
    own_query = ((pick_row == 0) & (pick_col == 2 * dp)).astype(F32)
    own_passage = ((pick_row == 1) & (pick_col == 2 * dp + 1)).astype(F32)
    picked = jnp.dot(own_query, coef, precision=HIGHEST, preferred_element_type=F32) + lax.dot_general(
        own_passage, coef, (((1,), (1,)), ((), ())), precision=HIGHEST, preferred_element_type=F32
    )
    for t in range(4):
        cols = slice(t * 1024, (t + 1) * 1024)
        grads = jnp.dot(
            picked,
            units[:, :, cols].reshape(RANKS, 1024),
            precision=HIGHEST,
            preferred_element_type=F32,
        )
        grads_ref[0, :, cols] = grads[0:2]


def vmem(shape, dtype):
    return pltpu.VMEM(shape, dtype)


def local(
    tokens, routes, route_weights, w_gate, w_up, w_down, rms_gain, query_len, passage_len, positive, logit_scale
):
    in_vmem = pl.BlockSpec(memory_space=pltpu.VMEM)
    in_smem = pl.BlockSpec(memory_space=pltpu.SMEM)
    anywhere = pl.BlockSpec(memory_space=pl.ANY)
    dma = pltpu.SemaphoreType.DMA
    slots = 2 * PLANES
    layer_out, units = pl.pallas_call(
        moe_kernel,
        out_shape=(
            jax.ShapeDtypeStruct((TOK, D), BF16),
            jax.ShapeDtypeStruct((2, D), F32),
        ),
        in_specs=[in_vmem] * 4 + [in_smem] + [anywhere] * 3,
        out_specs=(in_vmem, in_vmem),
        scratch_shapes=[
            vmem((slots, HALF, D), BF16),
            vmem((slots, HALF, D), BF16),
            vmem((slots, HALF, D), BF16),
            vmem((slots, HALF, D), BF16),
            vmem((2, D, FF), BF16),
            vmem((2, D, FF), BF16),
            vmem((2, FF, D), BF16),
            vmem((2, D), F32),
            dma((4,)),
            dma((3,)),
            dma((3,)),
            dma((slots,)),
            dma((slots,)),
            dma((slots,)),
            dma((slots,)),
        ],
        compiler_params=pltpu.CompilerParams(
            collective_id=0, has_side_effects=True, vmem_limit_bytes=48 * 2**20
        ),
        name="moe",
    )(
        tokens,
        routes.T,
        route_weights.T,
        rms_gain[None],
        jnp.concatenate([query_len, passage_len]),
        w_gate,
        w_up,
        w_down,
    )
    grads = pl.pallas_call(
        loss_kernel,
        out_shape=jax.ShapeDtypeStruct((1, 2, D), F32),
        in_specs=[in_vmem, in_smem, in_smem],
        out_specs=in_vmem,
        scratch_shapes=[
            vmem((XS, 2, WIDE), F32),
            vmem((ZS, 8, WIDE), F32),
            dma((XS,)),
            dma((XS,)),
            dma((ZS // 2, 2, 3)),
            dma((ZS, 3)),
        ],
        compiler_params=pltpu.CompilerParams(
            collective_id=1, has_side_effects=True, vmem_limit_bytes=32 * 2**20
        ),
        name="loss",
    )(units, positive, logit_scale)
    return layer_out, grads


def solution(mesh):
    return jax.shard_map(
        local,
        mesh=mesh,
        in_specs=(
            P(("dp", "expert"), None),
            P(("dp", "expert"), None),
            P(("dp", "expert"), None),
            P("expert", None, None),
            P("expert", None, None),
            P("expert", None, None),
            P(),
            P(("dp", "expert")),
            P(("dp", "expert")),
            P("expert", "dp"),
            P("expert", "dp"),
        ),
        out_specs=(P(("dp", "expert"), None), P(("dp", "expert"), None, None)),
        check_vma=False,
    )
```

```python
import functools

import jax
import jax.numpy as jnp
from jax import lax
from jax.experimental import pallas as pl
from jax.experimental.pallas import tpu as pltpu
from jax.sharding import PartitionSpec as P

MESH = pl.DeviceIdType.MESH
HIGHEST = lax.Precision.HIGHEST
F32 = jnp.float32
BF16 = jnp.bfloat16

PLANES = 8
ZS = 12
XS = 4
CAP = 32
HALF = 16
TOK = 128
D = 4096
FF = 256
QLEN = 32
META = 128
WIDE = D + META
CUT = 17 * 128
SQUARE = 256
BLOCKS = ZS * XS
HOPS = ZS // 2
RANKS = 2 * ZS * XS

DY = (0, 1, -1, 2, -2, -1, 1, 0)
TWIN = (0, 2, 1, 4, 3, 5, 6, 7)
SOURCE = (0, 1, -1, 2, -2, 1, -1, 0)
PACK_ORDER = (3, 4, 1, 2, 5, 6, 0, 7)


def ring_gather(z, x, ex, piece, sems, between):
    a_send, a_recv, b_send, b_recv, ax_send, bx_send = sems
    started = []

    def along_x(step):
        return (z * XS + lax.rem(x + step, XS), ex)

    def along_z(side):
        return (lax.rem(z + side + ZS, ZS) * XS + x, ex)

    def block_of(side, step, turn):
        return lax.rem(z - side * step + ZS, ZS) * XS + lax.rem(x + turn, XS)

    def send(half, block, device, send_sem, recv_sem):
        copy = pltpu.make_async_remote_copy(
            piece(block, half),
            piece(block, half),
            send_sem,
            recv_sem.at[block],
            device_id=device,
            device_id_type=MESH,
        )
        copy.start()
        started.append(copy)

    def arrive(half, block, recv_sem):
        pltpu.make_async_copy(piece(block, half), piece(block, half), recv_sem.at[block]).wait()

    def hops(side, stream):
        return HOPS if (side == 1) == (stream % 2 == 0) else HOPS - 1

    def forward(side, step, stream):
        if step < hops(side, stream):
            turn = stream % XS
            place = (side + 1) // 2
            half, recv = (1, b_recv) if stream == XS else (0, a_recv)
            sem = b_send.at[step, place] if stream == XS else a_send.at[step, place, turn]
            send(half, block_of(side, step, turn), along_z(side), sem, recv)

    def spread(side, step):
        for k in range(1, XS):
            place = (side * step) % ZS
            send(1, block_of(side, step, 0), along_x(k), bx_send.at[place, k], b_recv)

    for stream in (XS, 0):
        for side in (1, -1):
            forward(side, 0, stream)
    for k in range(1, XS):
        send(0, block_of(1, 0, 0), along_x(k), ax_send.at[k], a_recv)
    spread(1, 0)
    for turn in range(1, XS):
        arrive(0, block_of(1, 0, turn), a_recv)
        for side in (1, -1):
            forward(side, 0, turn)
    between(0)
    for step in range(1, HOPS + 1):
        for side in (1, -1):
            if step <= hops(side, XS):
                arrive(1, block_of(side, step, 0), b_recv)
                forward(side, step, XS)
                spread(side, step)
        for turn in range(XS):
            for side in (1, -1):
                if step <= hops(side, turn):
                    arrive(0, block_of(side, step, turn), a_recv)
                    forward(side, step, turn)
        between(step)
    for step in range(ZS):
        for turn in range(1, XS):
            arrive(1, block_of(1, step, turn), b_recv)
    return started


def gather_sems():
    dma = pltpu.SemaphoreType.DMA
    return [dma((HOPS, 2, XS)), dma((BLOCKS,)), dma((HOPS, 2)), dma((BLOCKS,)), dma((XS,)), dma((ZS, XS))]


def greet_dp(barrier, z, x, ex):
    for step in range(1, XS):
        pl.semaphore_signal(
            barrier, inc=1, device_id=(z * XS + lax.rem(x + step, XS), ex), device_id_type=MESH
        )
    for side in (-1, 1):
        pl.semaphore_signal(
            barrier, inc=1, device_id=(lax.rem(z + side + ZS, ZS) * XS + x, ex), device_id_type=MESH
        )


def moe_kernel(
    tok_hbm,
    routes_ref,
    rw_ref,
    gain_ref,
    lens_ref,
    wg_ref,
    wu_ref,
    wd_ref,
    layer_ref,
    unit_ref,
    sbuf,
    rbuf,
    obuf,
    ret,
    own,
    far,
    theirs,
    got,
    tok_ref,
    vec,
    copy_sem,
    load_sem,
    cross_sem,
    swap_sem,
    lend_sem,
    lent_sem,
    part_sem,
    dsend_sem,
    drecv_sem,
    csend_sem,
    crecv_sem,
    *sems,
):
    dp = lax.axis_index("dp")
    ex = lax.axis_index("expert")
    plane, core = ex // 2, lax.rem(ex, 2)

    z, x = dp // XS, lax.rem(dp, XS)

    def peer(offset, its_core):
        return (dp, lax.rem(plane + offset + PLANES, PLANES) * 2 + its_core)

    partner = peer(0, 1 - core)
    opposite = peer(PLANES // 2, core)
    barrier = pltpu.get_barrier_semaphore()
    for offset in (1, -1, 2, -2):
        for half in range(2):
            pl.semaphore_signal(barrier, inc=1, device_id=peer(offset, half), device_id_type=MESH)
    for device in (partner, opposite):
        pl.semaphore_signal(barrier, inc=1, device_id=device, device_id_type=MESH)
    greet_dp(barrier, z, x, ex)

    load_tokens = pltpu.make_async_copy(tok_hbm, tok_ref, copy_sem.at[2])
    loads = [
        pltpu.make_async_copy(wg_ref, own.at[core, pl.ds(0, 16)], load_sem.at[0]),
        pltpu.make_async_copy(wu_ref, own.at[core, pl.ds(16, 16)], load_sem.at[1]),
    ] + [
        pltpu.make_async_copy(
            wd_ref.at[0, :, pl.ds(i * SQUARE, SQUARE)], own.at[core, 32 + i], load_sem.at[2 + i]
        )
        for i in range(16)
    ]
    for copy in loads:
        copy.start()
    load_tokens.start()

    route0 = routes_ref[0:1, :]
    route1 = routes_ref[1:2, :]
    experts = lax.broadcasted_iota(jnp.int32, (8, TOK), 0)
    named = ((route0 == experts) | (route1 == experts)).astype(F32)
    earlier = (
        lax.broadcasted_iota(jnp.int32, (TOK, TOK), 0) < lax.broadcasted_iota(jnp.int32, (TOK, TOK), 1)
    ).astype(BF16)
    slot = jnp.dot(named.astype(BF16), earlier, preferred_element_type=F32)
    row = lax.broadcasted_iota(jnp.int32, (PLANES * CAP, 1), 0)
    place = row // CAP
    offset_of = jnp.where(place % 2 == 1, (place + 1) // 2, (PLANES - place // 2) % PLANES)
    expert_of = (plane + offset_of) % PLANES
    spread = (expert_of == lax.broadcasted_iota(jnp.int32, (PLANES * CAP, 8), 1)).astype(BF16)
    slot_of = jnp.dot(spread, slot.astype(BF16), preferred_element_type=F32)
    fits = slot_of == (row % CAP).astype(F32)
    hot0 = (fits & (route0 == expert_of)).astype(F32)
    hot1 = (fits & (route1 == expert_of)).astype(F32)
    hot = (hot0 + hot1).astype(BF16)
    blend = (hot0 * rw_ref[0:1, :] + hot1 * rw_ref[1:2, :]).T
    blend_high = blend.astype(BF16)
    blend_low = (blend - blend_high.astype(F32)).astype(BF16)

    for copy in loads:
        copy.wait()
    pl.semaphore_wait(barrier, 10 + XS + 1)
    cross = pltpu.make_async_remote_copy(
        own.at[core, dp],
        far.at[dp],
        cross_sem.at[0],
        cross_sem.at[1],
        device_id=opposite,
        device_id_type=MESH,
    )
    cross.start()
    load_tokens.wait()

    def to_partner(src, dst, send_sem, recv_sem):
        return pltpu.make_async_remote_copy(
            src, dst, send_sem, recv_sem, device_id=partner, device_id_type=MESH
        )

    def dispatch(p, half):
        return pltpu.make_async_remote_copy(
            sbuf.at[2 * p + half],
            rbuf.at[2 * TWIN[p] + core],
            dsend_sem.at[2 * p + half],
            drecv_sem.at[2 * TWIN[p] + core],
            device_id=peer(DY[p], half),
            device_id_type=MESH,
        )

    def give_back(q, half):
        return pltpu.make_async_remote_copy(
            obuf.at[2 * q + half],
            ret.at[2 * TWIN[q] + core],
            csend_sem.at[2 * q + half],
            crecv_sem.at[2 * TWIN[q] + core],
            device_id=peer(SOURCE[q], half),
            device_id_type=MESH,
        )

    def within(p, src, dst, send_sem, recv_sem):
        keep = pltpu.make_async_copy(src.at[2 * p + core], dst.at[2 * p + core], copy_sem.at[p // 7])
        give = to_partner(
            src.at[2 * p + 1 - core], dst.at[2 * p + core], send_sem.at[2 * p], recv_sem.at[2 * p]
        )
        return keep, give

    staying = [copy for p in (0, 7) for copy in within(p, sbuf, rbuf, dsend_sem, drecv_sem)]
    for p in PACK_ORDER:
        rows = jnp.dot(hot[p * CAP : (p + 1) * CAP], tok_ref[...], preferred_element_type=F32).astype(BF16)
        sbuf[2 * p : 2 * p + 2] = rows.reshape(2, HALF, D)
        if p not in (0, 7):
            for half in range(2):
                dispatch(p, half).start()
    for copy in staying:
        copy.start()
    swap = to_partner(own.at[core], own.at[core], swap_sem.at[0], swap_sem.at[1])
    swap.start()

    def arrived(ref, sem, i):
        pltpu.make_async_copy(ref.at[i], ref.at[i], sem.at[i]).wait()

    def activate(rows, gate_block, up_block):
        gate = jnp.dot(rows(), gate_block(), preferred_element_type=F32)
        up = jnp.dot(rows(), up_block(), preferred_element_type=F32)
        return (gate / (1.0 + jnp.exp(-gate)) * up).astype(BF16)

    def expand(low, high, h):
        return activate(
            lambda: rbuf[2 * low : 2 * high].reshape((high - low) * CAP, D),
            lambda: own[h, 0:16].reshape(D, FF),
            lambda: own[h, 16:32].reshape(D, FF),
        )

    def reduce(low, high, hidden):
        for t in range(16):
            cols = slice(t * SQUARE, (t + 1) * SQUARE)
            part0 = jnp.dot(hidden[0], own[0, 32 + t], preferred_element_type=F32).astype(BF16)
            part1 = jnp.dot(hidden[1], own[1, 32 + t], preferred_element_type=F32).astype(BF16)
            total = (part0.astype(F32) + part1.astype(F32)).astype(BF16)
            obuf[2 * low : 2 * high, :, cols] = total.reshape(2 * (high - low), HALF, SQUARE)
        for q in range(low, high):
            if q:
                for half in range(2):
                    give_back(q, half).start()

    lend = [
        to_partner(rbuf.at[10 + i], rbuf.at[16 + i], lend_sem.at[i], lent_sem.at[i]) for i in range(6)
    ]
    state = {}

    def between(step):
        if step == 2:
            swap.wait()
            for i in range(6, 10):
                arrived(rbuf, drecv_sem, i)
            state["far"] = [expand(3, 5, h) for h in range(2)]
        elif step == 3:
            reduce(3, 5, state["far"])
            for copy in staying:
                copy.wait()
            for i in range(2, 6):
                arrived(rbuf, drecv_sem, i)
            state["near"] = [expand(0, 3, 0)]
        elif step == 4:
            state["near"].append(expand(0, 3, 1))
            reduce(0, 3, state["near"])
        elif step == 5:
            for i in range(10, 14):
                arrived(rbuf, drecv_sem, i)
            for copy in lend:
                copy.start()

    cross.wait()

    def piece(block, half):
        return far.at[block, pl.ds(half * (SQUARE // 2), SQUARE // 2)]

    started = ring_gather(z, x, ex, piece, sems, between)
    for copy in lend:
        copy.wait()
    hidden = activate(
        lambda: rbuf[10:22].reshape(12 * HALF, D),
        lambda: far[0:16].reshape(D, FF),
        lambda: far[16:32].reshape(D, FF),
    )
    for t in range(16):
        cols = slice(t * SQUARE, (t + 1) * SQUARE)
        part = jnp.dot(hidden, far[32 + t], preferred_element_type=F32).astype(BF16)
        obuf[10:16, :, cols] = part[: 6 * HALF].reshape(6, HALF, SQUARE)
        theirs[:, :, cols] = part[6 * HALF :].reshape(6, HALF, SQUARE)
    parts = to_partner(theirs, got, part_sem.at[0], part_sem.at[1])
    parts.start()
    parts.wait()
    for i in (0, 2, 4):
        total = obuf[10 + i : 12 + i].astype(F32) + got[i : i + 2].astype(F32)
        obuf[10 + i : 12 + i] = total.astype(BF16)
        if i < 4:
            for half in range(2):
                give_back(5 + i // 2, half).start()
    returning = [copy for q in (0, 7) for copy in within(q, obuf, ret, csend_sem, crecv_sem)]
    for copy in returning:
        copy.start()

    for copy in started:
        copy.wait_send()
    for p in range(1, 7):
        for half in range(2):
            dispatch(p, half).wait_send()
            give_back(p, half).wait_send()
    for copy in returning:
        copy.wait()
    for i in range(2, 14):
        arrived(ret, crecv_sem, i)

    squares = jnp.zeros((TOK, 1), F32)
    for t in range(8):
        cols = slice(t * 512, (t + 1) * 512)
        outs = ret[:, :, cols].reshape(PLANES * CAP, 512)
        mixed = jnp.dot(blend_high, outs, preferred_element_type=F32) + jnp.dot(
            blend_low, outs, preferred_element_type=F32
        )
        block = (tok_ref[:, cols].astype(F32) + mixed).astype(BF16)
        layer_ref[:, cols] = block
        lifted = block.astype(F32)
        squares += jnp.sum(lifted * lifted, axis=1, keepdims=True)
    scale = lax.rsqrt(squares / D + 1e-05)
    position = lax.broadcasted_iota(jnp.int32, (TOK, 1), 0)
    q_len, p_len = lens_ref[0], lens_ref[1]
    q_coef = jnp.where(position < q_len, scale, 0.0) / q_len.astype(F32)
    p_coef = jnp.where((position >= QLEN) & (position < QLEN + p_len), scale, 0.0) / p_len.astype(F32)
    q_sum = jnp.zeros((1, 1), F32)
    p_sum = jnp.zeros((1, 1), F32)
    for t in range(8):
        cols = slice(t * 512, (t + 1) * 512)
        lifted = layer_ref[:, cols].astype(F32)
        gain = gain_ref[:, cols]
        q_vec = jnp.sum(lifted[:QLEN] * q_coef[:QLEN], axis=0, keepdims=True) * gain
        p_vec = jnp.sum(lifted[QLEN:] * p_coef[QLEN:], axis=0, keepdims=True) * gain
        q_sum += jnp.sum(q_vec * q_vec, axis=1, keepdims=True)
        p_sum += jnp.sum(p_vec * p_vec, axis=1, keepdims=True)
        vec[0:1, cols] = q_vec
        vec[1:2, cols] = p_vec
    unit_ref[0:1, :] = vec[0:1, :] * lax.rsqrt(q_sum + 1e-06)
    unit_ref[1:2, :] = vec[1:2, :] * lax.rsqrt(p_sum + 1e-06)


def loss_kernel(unit_ref, positive_ref, sharp_ref, grads_ref, line, units, *sems):
    dp = lax.axis_index("dp")
    ex = lax.axis_index("expert")
    z, x = dp // XS, lax.rem(dp, XS)
    barrier = pltpu.get_barrier_semaphore()
    greet_dp(barrier, z, x, ex)

    lane = lax.broadcasted_iota(jnp.int32, (2, META), 1)
    line[dp, :, 0:D] = unit_ref[...]
    line[dp, :, D:WIDE] = jnp.where(
        lane == 0, sharp_ref[0, 0], jnp.where(lane == 1, positive_ref[0, 0].astype(F32), 0.0)
    )
    pl.semaphore_wait(barrier, XS + 1)

    def piece(block, half):
        return line.at[block, :, pl.ds(CUT, WIDE - CUT) if half else pl.ds(0, CUT)]

    started = ring_gather(z, x, ex, piece, sems, lambda step: None)

    def merge(group, carry):
        for i in range(XS):
            units[group, 2 * i : 2 * i + 2, :] = line[XS * group + i]
        return carry

    lax.fori_loop(0, ZS, merge, 0)
    for copy in started:
        copy.wait_send()

    every = units[:, :, 0:D].reshape(RANKS, D)
    meta = units[:, :, D:WIDE].reshape(RANKS, META)
    sharp, positive = meta[:, 0:1], meta[:, 1:2]
    gram = lax.dot_general(
        every, every, (((1,), (1,)), ((), ())), precision=HIGHEST, preferred_element_type=F32
    )
    row = lax.broadcasted_iota(jnp.int32, (RANKS, RANKS), 0)
    col = lax.broadcasted_iota(jnp.int32, (RANKS, RANKS), 1)
    is_passage = col % 2 == 1
    scores = jnp.where(is_passage, gram * sharp, -jnp.inf)
    expos = jnp.exp(scores - jnp.max(scores, axis=1, keepdims=True))
    probs = expos / jnp.sum(expos, axis=1, keepdims=True)
    target = (is_passage & ((col // 2).astype(F32) == positive)).astype(F32)
    coef = jnp.where((row % 2 == 0) & is_passage, (probs - target) * sharp / (RANKS // 2), 0.0)
    pick_row = lax.broadcasted_iota(jnp.int32, (8, RANKS), 0)
    pick_col = lax.broadcasted_iota(jnp.int32, (8, RANKS), 1)
    own_query = ((pick_row == 0) & (pick_col == 2 * dp)).astype(F32)
    own_passage = ((pick_row == 1) & (pick_col == 2 * dp + 1)).astype(F32)
    picked = jnp.dot(own_query, coef, precision=HIGHEST, preferred_element_type=F32) + lax.dot_general(
        own_passage, coef, (((1,), (1,)), ((), ())), precision=HIGHEST, preferred_element_type=F32
    )
    for t in range(4):
        cols = slice(t * 1024, (t + 1) * 1024)
        grads = jnp.dot(
            picked,
            units[:, :, cols].reshape(RANKS, 1024),
            precision=HIGHEST,
            preferred_element_type=F32,
        )
        grads_ref[0, :, cols] = grads[0:2]


def vmem(shape, dtype):
    return pltpu.VMEM(shape, dtype)


def local(
    tokens, routes, route_weights, w_gate, w_up, w_down, rms_gain, query_len, passage_len, positive, logit_scale
):
    in_vmem = pl.BlockSpec(memory_space=pltpu.VMEM)
    in_smem = pl.BlockSpec(memory_space=pltpu.SMEM)
    anywhere = pl.BlockSpec(memory_space=pl.ANY)
    dma = pltpu.SemaphoreType.DMA
    slots = 2 * PLANES
    layer_out, units = pl.pallas_call(
        moe_kernel,
        out_shape=(
            jax.ShapeDtypeStruct((TOK, D), BF16),
            jax.ShapeDtypeStruct((2, D), F32),
        ),
        in_specs=[anywhere] + [in_vmem] * 3 + [in_smem] + [anywhere] * 3,
        out_specs=(in_vmem, in_vmem),
        scratch_shapes=[
            vmem((slots, HALF, D), BF16),
            vmem((slots + 6, HALF, D), BF16),
            vmem((slots, HALF, D), BF16),
            vmem((slots, HALF, D), BF16),
            vmem((2, BLOCKS, SQUARE, SQUARE), BF16),
            vmem((BLOCKS, SQUARE, SQUARE), BF16),
            vmem((6, HALF, D), BF16),
            vmem((6, HALF, D), BF16),
            vmem((TOK, D), BF16),
            vmem((2, D), F32),
            dma((3,)),
            dma((18,)),
            dma((2,)),
            dma((2,)),
            dma((6,)),
            dma((6,)),
            dma((2,)),
            dma((slots,)),
            dma((slots,)),
            dma((slots,)),
            dma((slots,)),
        ]
        + gather_sems(),
        compiler_params=pltpu.CompilerParams(
            collective_id=0, has_side_effects=True, vmem_limit_bytes=56 * 2**20
        ),
        name="moe",
    )(
        tokens,
        routes.T,
        route_weights.T,
        rms_gain[None],
        jnp.concatenate([query_len, passage_len]),
        w_gate.reshape(16, SQUARE, FF),
        w_up.reshape(16, SQUARE, FF),
        w_down,
    )
    grads = pl.pallas_call(
        loss_kernel,
        out_shape=jax.ShapeDtypeStruct((1, 2, D), F32),
        in_specs=[in_vmem, in_smem, in_smem],
        out_specs=in_vmem,
        scratch_shapes=[
            vmem((BLOCKS, 2, WIDE), F32),
            vmem((ZS, 8, WIDE), F32),
        ]
        + gather_sems(),
        compiler_params=pltpu.CompilerParams(
            collective_id=1, has_side_effects=True, vmem_limit_bytes=32 * 2**20
        ),
        name="loss",
    )(units, positive, logit_scale)
    return layer_out, grads


def solution(mesh):
    return jax.shard_map(
        local,
        mesh=mesh,
        in_specs=(
            P(("dp", "expert"), None),
            P(("dp", "expert"), None),
            P(("dp", "expert"), None),
            P("expert", None, None),
            P("expert", None, None),
            P("expert", None, None),
            P(),
            P(("dp", "expert")),
            P(("dp", "expert")),
            P("expert", "dp"),
            P("expert", "dp"),
        ),
        out_specs=(P(("dp", "expert"), None), P(("dp", "expert"), None, None)),
        check_vma=False,
    )
```

```python
import functools

import jax
import jax.numpy as jnp
from jax import lax
from jax.experimental import pallas as pl
from jax.experimental.pallas import tpu as pltpu
from jax.sharding import PartitionSpec as P

MESH = pl.DeviceIdType.MESH
HIGHEST = lax.Precision.HIGHEST
F32 = jnp.float32
BF16 = jnp.bfloat16

PLANES = 8
ZS = 12
XS = 4
CAP = 32
HALF = 16
TOK = 128
D = 4096
FF = 256
QLEN = 32
META = 128
WIDE = D + META
CUT = 8 * 128
WEIGHT_CUT = 96
SQUARE = 256
BLOCKS = ZS * XS
HOPS = ZS // 2
RANKS = 2 * ZS * XS

DY = (0, 1, -1, 2, -2, -1, 1, 0)
TWIN = (0, 2, 1, 4, 3, 5, 6, 7)
SOURCE = (0, 1, -1, 2, -2, 1, -1, 0)
PACK_ORDER = (3, 4, 1, 2, 5, 6, 0, 7)


def weight_gather(z, x, ex, blocks, crosses, sems, between):
    a_send, a_recv, b_send, b_recv, ax_send, bx_send, half_recv = sems
    started = []
    middle = (SQUARE - WEIGHT_CUT) // 2
    parts = (
        (0, WEIGHT_CUT),
        (WEIGHT_CUT, SQUARE - WEIGHT_CUT),
        (WEIGHT_CUT, middle),
        (WEIGHT_CUT + middle, middle),
    )

    def along_x(step):
        return (z * XS + lax.rem(x + step + XS, XS), ex)

    def along_z(side):
        return (lax.rem(z + side + ZS, ZS) * XS + x, ex)

    def block_of(side, step, turn):
        return lax.rem(z - side * step + ZS, ZS) * XS + lax.rem(x + turn + XS, XS)

    def piece(block, part):
        return blocks.at[block, pl.ds(*parts[part])]

    def send(part, block, device, send_sem, recv_sem):
        copy = pltpu.make_async_remote_copy(
            piece(block, part),
            piece(block, part),
            send_sem,
            recv_sem,
            device_id=device,
            device_id_type=MESH,
        )
        copy.start()
        started.append(copy)

    def arrive(part, block, recv_sem):
        pltpu.make_async_copy(piece(block, part), piece(block, part), recv_sem).wait()

    def hops(side, stream):
        return HOPS if (side == 1) == (stream % 2 == 0) else HOPS - 1

    def forward(side, step, stream):
        if step < hops(side, stream):
            turn = stream % XS
            place = (side + 1) // 2
            block = block_of(side, step, turn)
            if stream == XS:
                send(1, block, along_z(side), b_send.at[step, place], b_recv.at[block])
            else:
                send(0, block, along_z(side), a_send.at[step, place, turn], a_recv.at[block])

    def spread(side, step):
        block = block_of(side, step, 0)
        place = (side * step) % ZS
        for i, turn in enumerate((1, -1)):
            send(1, block, along_x(turn), bx_send.at[place, i], b_recv.at[block])

    def relay(side, step):
        place = (side * step) % ZS
        for i, turn in enumerate((1, -1)):
            block = block_of(side, step, -turn)
            arrive(1, block, b_recv.at[block])
            send(2 + i, block, along_x(turn), bx_send.at[place, 2 + i], half_recv.at[block, i])

    crosses[0].wait()
    for side in (1, -1):
        forward(side, 0, 0)
    for k in range(1, XS):
        block = block_of(1, 0, 0)
        send(0, block, along_x(k), ax_send.at[k], a_recv.at[block])
    crosses[1].wait()
    for side in (1, -1):
        forward(side, 0, XS)
    spread(1, 0)
    between(-1)
    for turn in range(1, XS):
        block = block_of(1, 0, turn)
        arrive(0, block, a_recv.at[block])
        for side in (1, -1):
            forward(side, 0, turn)
    between(0)
    for step in range(1, HOPS + 1):
        for side in (1, -1):
            if step <= hops(side, XS):
                block = block_of(side, step, 0)
                arrive(1, block, b_recv.at[block])
                forward(side, step, XS)
                spread(side, step)
        for turn in range(XS):
            for side in (1, -1):
                if step <= hops(side, turn):
                    block = block_of(side, step, turn)
                    arrive(0, block, a_recv.at[block])
                    forward(side, step, turn)
        for side in (1, -1):
            if step - 1 <= hops(side, XS) and (step > 1 or side == 1):
                relay(side, step - 1)
        between(step)
    relay(1, HOPS)
    for step in range(ZS):
        block = block_of(1, step, 2)
        for i in range(2):
            arrive(2 + i, block, half_recv.at[block, i])
    return started


def line_gather(z, x, ex, line, sems):
    a_send, a_recv, b_send, b_recv, ax_send, bx_send = sems
    started = []
    first = pl.ds(0, CUT)
    rest = pl.ds(CUT, WIDE - CUT)

    def along_x(step):
        return (z * XS + lax.rem(x + step, XS), ex)

    def level(distance):
        return lax.rem(z - distance + ZS, ZS)

    def send(ref, device, send_sem, recv_sem):
        copy = pltpu.make_async_remote_copy(
            ref, ref, send_sem, recv_sem, device_id=device, device_id_type=MESH
        )
        copy.start()
        started.append(copy)

    def arrive(ref, recv_sem):
        pltpu.make_async_copy(ref, ref, recv_sem).wait()

    def four(row):
        return line.at[pl.ds(row * XS, XS), :, first]

    def one(row, turn):
        return line.at[row * XS + lax.rem(x + turn, XS), :, rest]

    def limit(half, side):
        return HOPS if (half == 0) == (side == 1) else HOPS - 1

    def stride(half, side, distance):
        row = level(side * distance)
        for step in (2, 1):
            if distance + step <= limit(half, side):
                device = (lax.rem(z + side * step + ZS, ZS) * XS + x, ex)
                place = (distance // 2, (side + 1) // 2, step - 1)
                if half:
                    send(one(row, 0), device, b_send.at[place], b_recv.at[row * XS + x])
                else:
                    send(four(row), device, a_send.at[place], a_recv.at[row])

    def spread(distance):
        row = level(distance)
        for k in range(1, XS):
            send(one(row, 0), along_x(k), bx_send.at[distance % ZS, k], b_recv.at[row * XS + x])

    own = line.at[z * XS + x, :, first]
    for k in range(1, XS):
        send(own, along_x(k), ax_send.at[k], a_recv.at[ZS + x])
    for side in (1, -1):
        stride(1, side, 0)
    spread(0)
    for turn in range(1, XS):
        column = lax.rem(x + turn, XS)
        arrive(line.at[z * XS + column, :, first], a_recv.at[ZS + column])
    for side in (1, -1):
        stride(0, side, 0)
    for trip in range(HOPS // 2):
        came = []
        for step in (2, 1):
            for half in (1, 0):
                for side in (1, -1):
                    distance = 2 * trip + step
                    if distance <= limit(half, side):
                        row = level(side * distance)
                        if half:
                            arrive(one(row, 0), b_recv.at[row * XS + x])
                            came.append(side * distance)
                        else:
                            arrive(four(row), a_recv.at[row])
                        if step == 2:
                            stride(half, side, distance)
            for distance in came:
                spread(distance)
            came = []
    for step in range(ZS):
        row = level(step)
        for turn in range(1, XS):
            arrive(one(row, turn), b_recv.at[row * XS + lax.rem(x + turn, XS)])
    return started


def weight_sems():
    dma = pltpu.SemaphoreType.DMA
    return [
        dma((HOPS, 2, XS)),
        dma((BLOCKS,)),
        dma((HOPS, 2)),
        dma((BLOCKS,)),
        dma((XS,)),
        dma((ZS, 4)),
        dma((BLOCKS, 2)),
    ]


def line_sems():
    dma = pltpu.SemaphoreType.DMA
    return [dma((3, 2, 2)), dma((ZS + XS,)), dma((3, 2, 2)), dma((BLOCKS,)), dma((XS,)), dma((ZS, XS))]


def greet_dp(barrier, z, x, ex):
    for step in range(1, XS):
        pl.semaphore_signal(
            barrier, inc=1, device_id=(z * XS + lax.rem(x + step, XS), ex), device_id_type=MESH
        )
    for side in (-2, -1, 1, 2):
        pl.semaphore_signal(
            barrier, inc=1, device_id=(lax.rem(z + side + ZS, ZS) * XS + x, ex), device_id_type=MESH
        )


def moe_kernel(
    tok_hbm,
    mixed_ref,
    wg_ref,
    wu_ref,
    wd_ref,
    layer_ref,
    grads_ref,
    sbuf,
    rbuf,
    obuf,
    ret,
    own,
    far,
    theirs,
    got,
    tok_ref,
    line,
    units,
    split,
    copy_sem,
    load_sem,
    cross_sem,
    swap_sem,
    lend_sem,
    lent_sem,
    part_sem,
    dsend_sem,
    drecv_sem,
    csend_sem,
    crecv_sem,
    fsend_sem,
    frecv_sem,
    *sems,
):
    dp = lax.axis_index("dp")
    ex = lax.axis_index("expert")
    plane, core = ex // 2, lax.rem(ex, 2)

    z, x = dp // XS, lax.rem(dp, XS)

    def peer(offset, its_core):
        return (dp, lax.rem(plane + offset + PLANES, PLANES) * 2 + its_core)

    partner = peer(0, 1 - core)
    opposite = peer(PLANES // 2, core)
    barrier = pltpu.get_barrier_semaphore()
    for offset in (1, -1, 2, -2):
        for half in range(2):
            pl.semaphore_signal(barrier, inc=1, device_id=peer(offset, half), device_id_type=MESH)
    for device in (partner, opposite):
        pl.semaphore_signal(barrier, inc=1, device_id=device, device_id_type=MESH)
    greet_dp(barrier, z, x, ex)

    load_tokens = pltpu.make_async_copy(tok_hbm, tok_ref, copy_sem.at[2])
    loads = [
        pltpu.make_async_copy(wg_ref, own.at[core, pl.ds(0, 16)], load_sem.at[0]),
        pltpu.make_async_copy(wu_ref, own.at[core, pl.ds(16, 16)], load_sem.at[1]),
    ] + [
        pltpu.make_async_copy(
            wd_ref.at[0, :, pl.ds(i * SQUARE, SQUARE)], own.at[core, 32 + i], load_sem.at[2 + i]
        )
        for i in range(16)
    ]
    for copy in loads:
        copy.start()
    load_tokens.start()

    route0 = mixed_ref[1:2, 0:TOK].astype(jnp.int32)
    route1 = mixed_ref[2:3, 0:TOK].astype(jnp.int32)
    scalars = mixed_ref[5:6, 0:TOK]
    experts = lax.broadcasted_iota(jnp.int32, (8, TOK), 0)
    named = ((route0 == experts) | (route1 == experts)).astype(F32)
    earlier = (
        lax.broadcasted_iota(jnp.int32, (TOK, TOK), 0) < lax.broadcasted_iota(jnp.int32, (TOK, TOK), 1)
    ).astype(BF16)
    slot = jnp.dot(named.astype(BF16), earlier, preferred_element_type=F32)
    row = lax.broadcasted_iota(jnp.int32, (PLANES * CAP, 1), 0)
    place = row // CAP
    offset_of = jnp.where(place % 2 == 1, (place + 1) // 2, (PLANES - place // 2) % PLANES)
    expert_of = (plane + offset_of) % PLANES
    spread = (expert_of == lax.broadcasted_iota(jnp.int32, (PLANES * CAP, 8), 1)).astype(BF16)
    slot_of = jnp.dot(spread, slot.astype(BF16), preferred_element_type=F32)
    fits = slot_of == (row % CAP).astype(F32)
    hot0 = (fits & (route0 == expert_of)).astype(F32)
    hot1 = (fits & (route1 == expert_of)).astype(F32)
    hot = (hot0 + hot1).astype(BF16)
    blend = (hot0 * mixed_ref[3:4, 0:TOK] + hot1 * mixed_ref[4:5, 0:TOK]).T
    blend_high = blend.astype(BF16)
    blend_low = (blend - blend_high.astype(F32)).astype(BF16)

    for copy in loads:
        copy.wait()
    pl.semaphore_wait(barrier, 10 + XS + 3)
    crosses = [
        pltpu.make_async_remote_copy(
            own.at[core, dp, rows],
            far.at[dp, rows],
            cross_sem.at[0, i],
            cross_sem.at[1, i],
            device_id=opposite,
            device_id_type=MESH,
        )
        for i, rows in enumerate((pl.ds(0, WEIGHT_CUT), pl.ds(WEIGHT_CUT, SQUARE - WEIGHT_CUT)))
    ]
    for copy in crosses:
        copy.start()
    load_tokens.wait()

    def to_partner(src, dst, send_sem, recv_sem):
        return pltpu.make_async_remote_copy(
            src, dst, send_sem, recv_sem, device_id=partner, device_id_type=MESH
        )

    def dispatch(p, half):
        return pltpu.make_async_remote_copy(
            sbuf.at[2 * p + half],
            rbuf.at[2 * TWIN[p] + core],
            dsend_sem.at[2 * p + half],
            drecv_sem.at[2 * TWIN[p] + core],
            device_id=peer(DY[p], half),
            device_id_type=MESH,
        )

    def give_back(q, half):
        return pltpu.make_async_remote_copy(
            obuf.at[2 * q + half],
            ret.at[2 * TWIN[q] + core],
            csend_sem.at[2 * q + half],
            crecv_sem.at[2 * TWIN[q] + core],
            device_id=peer(SOURCE[q], half),
            device_id_type=MESH,
        )

    def within(p, src, dst, send_sem, recv_sem):
        keep = pltpu.make_async_copy(src.at[2 * p + core], dst.at[2 * p + core], copy_sem.at[p // 7])
        give = to_partner(
            src.at[2 * p + 1 - core], dst.at[2 * p + core], send_sem.at[2 * p], recv_sem.at[2 * p]
        )
        return keep, give

    staying = [copy for p in (0, 7) for copy in within(p, sbuf, rbuf, dsend_sem, drecv_sem)]
    for p in PACK_ORDER:
        rows = jnp.dot(hot[p * CAP : (p + 1) * CAP], tok_ref[...], preferred_element_type=F32).astype(BF16)
        sbuf[2 * p : 2 * p + 2] = rows.reshape(2, HALF, D)
    for copy in staying:
        copy.start()
    swap = to_partner(own.at[core], own.at[core], swap_sem.at[0], swap_sem.at[1])
    swap.start()

    def arrived(ref, sem, i):
        pltpu.make_async_copy(ref.at[i], ref.at[i], sem.at[i]).wait()

    def activate(rows, gate_block, up_block):
        gate = jnp.dot(rows(), gate_block(), preferred_element_type=F32)
        up = jnp.dot(rows(), up_block(), preferred_element_type=F32)
        return (gate / (1.0 + jnp.exp(-gate)) * up).astype(BF16)

    def expand(low, high, h):
        return activate(
            lambda: rbuf[2 * low : 2 * high].reshape((high - low) * CAP, D),
            lambda: own[h, 0:16].reshape(D, FF),
            lambda: own[h, 16:32].reshape(D, FF),
        )

    def reduce(low, high, hidden):
        for t in range(16):
            cols = slice(t * SQUARE, (t + 1) * SQUARE)
            part0 = jnp.dot(hidden[0], own[0, 32 + t], preferred_element_type=F32).astype(BF16)
            part1 = jnp.dot(hidden[1], own[1, 32 + t], preferred_element_type=F32).astype(BF16)
            total = (part0.astype(F32) + part1.astype(F32)).astype(BF16)
            obuf[2 * low : 2 * high, :, cols] = total.reshape(2 * (high - low), HALF, SQUARE)
        for q in range(low, high):
            if q:
                for half in range(2):
                    give_back(q, half).start()

    lend = [
        to_partner(rbuf.at[10 + i], rbuf.at[16 + i], lend_sem.at[i], lent_sem.at[i]) for i in range(6)
    ]
    state = {}

    def between(step):
        if step == -1:
            for p in PACK_ORDER[:6]:
                for half in range(2):
                    dispatch(p, half).start()
        elif step == 2:
            swap.wait()
            for i in range(6, 10):
                arrived(rbuf, drecv_sem, i)
            state["far"] = [expand(3, 5, h) for h in range(2)]
        elif step == 3:
            reduce(3, 5, state["far"])
            for copy in staying:
                copy.wait()
            for i in range(2, 6):
                arrived(rbuf, drecv_sem, i)
            state["near"] = [expand(0, 3, 0)]
        elif step == 4:
            state["near"].append(expand(0, 3, 1))
            reduce(0, 3, state["near"])
        elif step == 5:
            for i in range(10, 14):
                arrived(rbuf, drecv_sem, i)
            for copy in lend:
                copy.start()

    started = weight_gather(z, x, ex, far, crosses, sems[:7], between)
    for copy in lend:
        copy.wait()
    hidden = activate(
        lambda: rbuf[10:22].reshape(12 * HALF, D),
        lambda: far[0:16].reshape(D, FF),
        lambda: far[16:32].reshape(D, FF),
    )
    quarter = D // 4
    parts = []
    for t in range(4):
        for i in range(4):
            cols = slice(t * quarter + i * SQUARE, t * quarter + (i + 1) * SQUARE)
            part = jnp.dot(hidden, far[32 + 4 * t + i], preferred_element_type=F32).astype(BF16)
            obuf[10:16, :, cols] = part[: 6 * HALF].reshape(6, HALF, SQUARE)
            theirs[:, :, cols] = part[6 * HALF :].reshape(6, HALF, SQUARE)
        whole = pl.ds(t * quarter, quarter)
        parts.append(
            to_partner(theirs.at[:, :, whole], got.at[:, :, whole], part_sem.at[0, t], part_sem.at[1, t])
        )
        parts[t].start()
    returning = []
    for t in range(4):
        parts[t].wait()
        cols = slice(t * quarter, (t + 1) * quarter)
        whole = pl.ds(t * quarter, quarter)
        for i in (0, 2, 4):
            total = obuf[10 + i : 12 + i, :, cols].astype(F32) + got[i : i + 2, :, cols].astype(F32)
            obuf[10 + i : 12 + i, :, cols] = total.astype(BF16)
            if i < 4:
                for half in range(2):
                    q = 5 + i // 2
                    returning.append(
                        pltpu.make_async_remote_copy(
                            obuf.at[2 * q + half, :, whole],
                            ret.at[2 * q + core, :, whole],
                            fsend_sem.at[t, i + half],
                            frecv_sem.at[t, i + core],
                            device_id=peer(SOURCE[q], half),
                            device_id_type=MESH,
                        )
                    )
                    returning[-1].start()
    final = [copy for q in (0, 7) for copy in within(q, obuf, ret, csend_sem, crecv_sem)]
    for copy in final:
        copy.start()

    for copy in started:
        copy.wait_send()
    for p in range(1, 7):
        for half in range(2):
            dispatch(p, half).wait_send()
            if p < 5:
                give_back(p, half).wait_send()
    for copy in final:
        copy.wait()
    for i in range(2, 10):
        arrived(ret, crecv_sem, i)
    for copy in returning:
        copy.wait_send()
    for t in range(4):
        whole = pl.ds(t * quarter, quarter)
        for i in range(4):
            pltpu.make_async_copy(
                ret.at[10 + i, :, whole], ret.at[10 + i, :, whole], frecv_sem.at[t, i]
            ).wait()

    squares = jnp.zeros((TOK, 1), F32)
    for t in range(8):
        cols = slice(t * 512, (t + 1) * 512)
        outs = ret[:, :, cols].reshape(PLANES * CAP, 512)
        mixed = jnp.dot(blend_high, outs, preferred_element_type=F32) + jnp.dot(
            blend_low, outs, preferred_element_type=F32
        )
        block = (tok_ref[:, cols].astype(F32) + mixed).astype(BF16)
        layer_ref[:, cols] = block
        lifted = block.astype(F32)
        squares += jnp.sum(lifted * lifted, axis=1, keepdims=True)
    scale = lax.rsqrt(squares / D + 1e-05)
    position = lax.broadcasted_iota(jnp.int32, (TOK, 1), 0).astype(F32)
    q_len, p_len = scalars[:, 0:1], scalars[:, 1:2]
    q_coef = jnp.where(position < q_len, scale, 0.0) / q_len
    p_coef = jnp.where((position >= QLEN) & (position < QLEN + p_len), scale, 0.0) / p_len
    q_sum = jnp.zeros((1, 1), F32)
    p_sum = jnp.zeros((1, 1), F32)
    for t in range(8):
        cols = slice(t * 512, (t + 1) * 512)
        lifted = layer_ref[:, cols].astype(F32)
        gain = mixed_ref[0:1, cols]
        q_vec = jnp.sum(lifted[:QLEN] * q_coef[:QLEN], axis=0, keepdims=True) * gain
        p_vec = jnp.sum(lifted[QLEN:] * p_coef[QLEN:], axis=0, keepdims=True) * gain
        q_sum += jnp.sum(q_vec * q_vec, axis=1, keepdims=True)
        p_sum += jnp.sum(p_vec * p_vec, axis=1, keepdims=True)
        line[dp, 0:1, cols] = q_vec
        line[dp, 1:2, cols] = p_vec
    kind = lax.broadcasted_iota(jnp.int32, (2, 1), 0)
    line[dp, :, 0:D] = line[dp, :, 0:D] * lax.rsqrt(jnp.where(kind == 0, q_sum, p_sum) + 1e-06)
    lane = lax.broadcasted_iota(jnp.int32, (2, META), 1)
    line[dp, :, D:WIDE] = jnp.where(
        lane == 0, scalars[:, 3:4], jnp.where(lane == 1, scalars[:, 2:3], 0.0)
    )
    started = line_gather(z, x, ex, line, sems[7:])

    def merge(group, carry):
        for i in range(XS):
            units[group, 2 * i : 2 * i + 2, :] = line[XS * group + i]
        return carry

    lax.fori_loop(0, ZS, merge, 0)

    def divide(group, carry):
        rows = units[pl.ds(2 * group, 2), :, 0:D].reshape(16, D)
        high = rows.astype(BF16)
        split[0, group] = high
        split[1, group] = (rows - high.astype(F32)).astype(BF16)
        return carry

    lax.fori_loop(0, ZS // 2, divide, 0)
    for copy in started:
        copy.wait_send()

    meta = units[:, :, D:WIDE].reshape(RANKS, META)
    sharp, positive = meta[:, 0:1], meta[:, 1:2]
    across = (((1,), (1,)), ((), ()))
    high_gram = lax.dot_general(
        split[...].reshape(2 * RANKS, D), split[0].reshape(RANKS, D), across, preferred_element_type=F32
    )
    low_gram = lax.dot_general(
        split[0].reshape(RANKS, D), split[1].reshape(RANKS, D), across, preferred_element_type=F32
    )
    gram = high_gram[:RANKS] + (high_gram[RANKS:] + low_gram)
    row = lax.broadcasted_iota(jnp.int32, (RANKS, RANKS), 0)
    col = lax.broadcasted_iota(jnp.int32, (RANKS, RANKS), 1)
    is_passage = col % 2 == 1
    scores = jnp.where(is_passage, gram * sharp, -jnp.inf)
    expos = jnp.exp(scores - jnp.max(scores, axis=1, keepdims=True))
    probs = expos / jnp.sum(expos, axis=1, keepdims=True)
    target = (is_passage & ((col // 2).astype(F32) == positive)).astype(F32)
    coef = jnp.where((row % 2 == 0) & is_passage, (probs - target) * sharp / (RANKS // 2), 0.0)
    pick_row = lax.broadcasted_iota(jnp.int32, (8, RANKS), 0)
    pick_col = lax.broadcasted_iota(jnp.int32, (8, RANKS), 1)
    own_query = ((pick_row == 0) & (pick_col == 2 * dp)).astype(F32)
    own_passage = ((pick_row == 1) & (pick_col == 2 * dp + 1)).astype(F32)
    picked = jnp.dot(own_query, coef, precision=HIGHEST, preferred_element_type=F32) + lax.dot_general(
        own_passage, coef, (((1,), (1,)), ((), ())), precision=HIGHEST, preferred_element_type=F32
    )
    picked_high = picked.astype(BF16)
    picked_low = (picked - picked_high.astype(F32)).astype(BF16)
    both = jnp.concatenate([picked_high.astype(F32), picked_low.astype(F32)], axis=0).astype(BF16)
    for t in range(4):
        cols = slice(t * 1024, (t + 1) * 1024)
        top = jnp.dot(both, split[0, :, :, cols].reshape(RANKS, 1024), preferred_element_type=F32)
        low = jnp.dot(both, split[1, :, :, cols].reshape(RANKS, 1024), preferred_element_type=F32)
        grads_ref[0, :, cols] = top[0:2] + (top[8:10] + low[0:2])


def vmem(shape, dtype):
    return pltpu.VMEM(shape, dtype)


def local(
    tokens, routes, route_weights, w_gate, w_up, w_down, rms_gain, query_len, passage_len, positive, logit_scale
):
    in_vmem = pl.BlockSpec(memory_space=pltpu.VMEM)
    anywhere = pl.BlockSpec(memory_space=pl.ANY)
    dma = pltpu.SemaphoreType.DMA
    slots = 2 * PLANES
    places = [(0, 0, rms_gain[None]), (1, 0, routes.T.astype(F32)), (3, 0, route_weights.T)]
    for i, v in enumerate((query_len, passage_len, positive, logit_scale)):
        places.append((5, i, v.reshape(1, 1).astype(F32)))
    mixed = 0.0
    for row, column, v in places:
        mixed += jnp.pad(v, ((row, 8 - row - v.shape[0]), (column, D - column - v.shape[1])))
    return pl.pallas_call(
        moe_kernel,
        out_shape=(
            jax.ShapeDtypeStruct((TOK, D), BF16),
            jax.ShapeDtypeStruct((1, 2, D), F32),
        ),
        in_specs=[anywhere, in_vmem] + [anywhere] * 3,
        out_specs=(in_vmem, in_vmem),
        scratch_shapes=[
            vmem((slots, HALF, D), BF16),
            vmem((slots + 6, HALF, D), BF16),
            vmem((slots, HALF, D), BF16),
            vmem((slots, HALF, D), BF16),
            vmem((2, BLOCKS, SQUARE, SQUARE), BF16),
            vmem((BLOCKS, SQUARE, SQUARE), BF16),
            vmem((6, HALF, D), BF16),
            vmem((6, HALF, D), BF16),
            vmem((TOK, D), BF16),
            vmem((BLOCKS, 2, WIDE), F32),
            vmem((ZS, 8, WIDE), F32),
            vmem((2, ZS // 2, 16, D), BF16),
            dma((3,)),
            dma((18,)),
            dma((2, 2)),
            dma((2,)),
            dma((6,)),
            dma((6,)),
            dma((2, 4)),
            dma((slots,)),
            dma((slots,)),
            dma((slots,)),
            dma((slots,)),
            dma((4, 4)),
            dma((4, 4)),
        ]
        + weight_sems()
        + line_sems(),
        compiler_params=pltpu.CompilerParams(
            collective_id=0, has_side_effects=True, vmem_limit_bytes=52 * 2**20
        ),
        name="moe",
    )(
        tokens,
        mixed,
        w_gate.reshape(16, SQUARE, FF),
        w_up.reshape(16, SQUARE, FF),
        w_down,
    )


def solution(mesh):
    return jax.shard_map(
        local,
        mesh=mesh,
        in_specs=(
            P(("dp", "expert"), None),
            P(("dp", "expert"), None),
            P(("dp", "expert"), None),
            P("expert", None, None),
            P("expert", None, None),
            P("expert", None, None),
            P(),
            P(("dp", "expert")),
            P(("dp", "expert")),
            P("expert", "dp"),
            P("expert", "dp"),
        ),
        out_specs=(P(("dp", "expert"), None), P(("dp", "expert"), None, None)),
        check_vma=False,
    )
```

```python
import functools

import jax
import jax.numpy as jnp
from jax import lax
from jax.experimental import pallas as pl
from jax.experimental.pallas import tpu as pltpu
from jax.sharding import PartitionSpec as P

MESH = pl.DeviceIdType.MESH
HIGHEST = lax.Precision.HIGHEST
F32 = jnp.float32
BF16 = jnp.bfloat16

PLANES = 8
ZS = 12
XS = 4
CAP = 32
HALF = 16
TOK = 128
D = 4096
FF = 256
QLEN = 32
META = 128
WIDE = D + META
CUT = 8 * 128
WEIGHT_CUT = 96
SQUARE = 256
BLOCKS = ZS * XS
HOPS = ZS // 2
RANKS = 2 * ZS * XS

DY = (0, 1, -1, 2, -2, -1, 1, 0)
TWIN = (0, 2, 1, 4, 3, 5, 6, 7)
SOURCE = (0, 1, -1, 2, -2, 1, -1, 0)
PACK_ORDER = (3, 4, 1, 2, 5, 6, 0, 7)


def weight_gather(z, x, ex, blocks, crosses, sems, between):
    a_send, a_recv, b_send, b_recv, ax_send, bx_send, half_recv = sems
    started = []
    middle = (SQUARE - WEIGHT_CUT) // 2
    parts = (
        (0, WEIGHT_CUT),
        (WEIGHT_CUT, SQUARE - WEIGHT_CUT),
        (WEIGHT_CUT, middle),
        (WEIGHT_CUT + middle, middle),
    )

    def along_x(step):
        return (z * XS + lax.rem(x + step + XS, XS), ex)

    def along_z(side):
        return (lax.rem(z + side + ZS, ZS) * XS + x, ex)

    def block_of(side, step, turn):
        return lax.rem(z - side * step + ZS, ZS) * XS + lax.rem(x + turn + XS, XS)

    def piece(block, part):
        return blocks.at[block, pl.ds(*parts[part])]

    def send(part, block, device, send_sem, recv_sem):
        copy = pltpu.make_async_remote_copy(
            piece(block, part),
            piece(block, part),
            send_sem,
            recv_sem,
            device_id=device,
            device_id_type=MESH,
        )
        copy.start()
        started.append(copy)

    def arrive(part, block, recv_sem):
        pltpu.make_async_copy(piece(block, part), piece(block, part), recv_sem).wait()

    def hops(side, stream):
        return HOPS if (side == 1) == (stream % 2 == 0) else HOPS - 1

    def forward(side, step, stream):
        if step < hops(side, stream):
            turn = stream % XS
            place = (side + 1) // 2
            block = block_of(side, step, turn)
            if stream == XS:
                send(1, block, along_z(side), b_send.at[step, place], b_recv.at[block])
            else:
                send(0, block, along_z(side), a_send.at[step, place, turn], a_recv.at[block])

    def spread(side, step):
        block = block_of(side, step, 0)
        place = (side * step) % ZS
        for i, turn in enumerate((1, -1, 2) if step == hops(side, XS) else (1, -1)):
            send(1, block, along_x(turn), bx_send.at[place, i], b_recv.at[block])

    def relay(side, step):
        place = (side * step) % ZS
        for i, turn in enumerate((1, -1)):
            block = block_of(side, step, -turn)
            arrive(1, block, b_recv.at[block])
            if step == hops(side, XS):
                continue
            send(2 + i, block, along_x(turn), bx_send.at[place, 2 + i], half_recv.at[block, i])

    crosses[0].wait()
    for side in (1, -1):
        forward(side, 0, 0)
    for k in range(1, XS):
        block = block_of(1, 0, 0)
        send(0, block, along_x(k), ax_send.at[k], a_recv.at[block])
    crosses[1].wait()
    for side in (1, -1):
        forward(side, 0, XS)
    spread(1, 0)
    between(-1)
    for turn in range(1, XS):
        block = block_of(1, 0, turn)
        arrive(0, block, a_recv.at[block])
        for side in (1, -1):
            forward(side, 0, turn)
    between(0)
    for step in range(1, HOPS + 1):
        for side in (1, -1):
            if step <= hops(side, XS):
                block = block_of(side, step, 0)
                arrive(1, block, b_recv.at[block])
                forward(side, step, XS)
                spread(side, step)
        for turn in range(XS):
            for side in (1, -1):
                if step <= hops(side, turn):
                    block = block_of(side, step, turn)
                    arrive(0, block, a_recv.at[block])
                    forward(side, step, turn)
        for side in (1, -1):
            if step - 1 <= hops(side, XS) and (step > 1 or side == 1):
                relay(side, step - 1)
        between(step)
    relay(1, HOPS)
    for step in range(ZS):
        block = block_of(1, step, 2)
        if step in (HOPS, HOPS + 1):
            arrive(1, block, b_recv.at[block])
            continue
        for i in range(2):
            arrive(2 + i, block, half_recv.at[block, i])
    return started


def line_gather(z, x, ex, line, sems):
    a_send, a_recv, b_send, b_recv, ax_send, bx_send = sems
    started = []
    first = pl.ds(0, CUT)
    rest = pl.ds(CUT, WIDE - CUT)

    def along_x(step):
        return (z * XS + lax.rem(x + step, XS), ex)

    def level(distance):
        return lax.rem(z - distance + ZS, ZS)

    def send(ref, device, send_sem, recv_sem):
        copy = pltpu.make_async_remote_copy(
            ref, ref, send_sem, recv_sem, device_id=device, device_id_type=MESH
        )
        copy.start()
        started.append(copy)

    def arrive(ref, recv_sem):
        pltpu.make_async_copy(ref, ref, recv_sem).wait()

    def four(row):
        return line.at[pl.ds(row * XS, XS), :, first]

    def one(row, turn):
        return line.at[row * XS + lax.rem(x + turn, XS), :, rest]

    def limit(half, side):
        return HOPS if (half == 0) == (side == 1) else HOPS - 1

    def stride(half, side, distance):
        row = level(side * distance)
        for step in (2, 1):
            if distance + step <= limit(half, side):
                device = (lax.rem(z + side * step + ZS, ZS) * XS + x, ex)
                place = (distance // 2, (side + 1) // 2, step - 1)
                if half:
                    send(one(row, 0), device, b_send.at[place], b_recv.at[row * XS + x])
                else:
                    send(four(row), device, a_send.at[place], a_recv.at[row])

    def spread(distance):
        row = level(distance)
        for k in range(1, XS):
            send(one(row, 0), along_x(k), bx_send.at[distance % ZS, k], b_recv.at[row * XS + x])

    own = line.at[z * XS + x, :, first]
    for k in range(1, XS):
        send(own, along_x(k), ax_send.at[k], a_recv.at[ZS + x])
    for side in (1, -1):
        stride(1, side, 0)
    spread(0)
    for turn in range(1, XS):
        column = lax.rem(x + turn, XS)
        arrive(line.at[z * XS + column, :, first], a_recv.at[ZS + column])
    for side in (1, -1):
        stride(0, side, 0)
    for trip in range(HOPS // 2):
        came = []
        for step in (2, 1):
            for half in (1, 0):
                for side in (1, -1):
                    distance = 2 * trip + step
                    if distance <= limit(half, side):
                        row = level(side * distance)
                        if half:
                            arrive(one(row, 0), b_recv.at[row * XS + x])
                            came.append(side * distance)
                        else:
                            arrive(four(row), a_recv.at[row])
                        if step == 2:
                            stride(half, side, distance)
            for distance in came:
                spread(distance)
            came = []
    for step in range(ZS):
        row = level(step)
        for turn in range(1, XS):
            arrive(one(row, turn), b_recv.at[row * XS + lax.rem(x + turn, XS)])
    return started


def weight_sems():
    dma = pltpu.SemaphoreType.DMA
    return [
        dma((HOPS, 2, XS)),
        dma((BLOCKS,)),
        dma((HOPS, 2)),
        dma((BLOCKS,)),
        dma((XS,)),
        dma((ZS, 4)),
        dma((BLOCKS, 2)),
    ]


def line_sems():
    dma = pltpu.SemaphoreType.DMA
    return [dma((3, 2, 2)), dma((ZS + XS,)), dma((3, 2, 2)), dma((BLOCKS,)), dma((XS,)), dma((ZS, XS))]


def greet_dp(barrier, z, x, ex):
    for step in range(1, XS):
        pl.semaphore_signal(
            barrier, inc=1, device_id=(z * XS + lax.rem(x + step, XS), ex), device_id_type=MESH
        )
    for side in (-2, -1, 1, 2):
        pl.semaphore_signal(
            barrier, inc=1, device_id=(lax.rem(z + side + ZS, ZS) * XS + x, ex), device_id_type=MESH
        )


def moe_kernel(
    tok_hbm,
    mixed_ref,
    wg_ref,
    wu_ref,
    wd_ref,
    layer_ref,
    grads_ref,
    sbuf,
    rbuf,
    obuf,
    ret,
    own,
    far,
    theirs,
    got,
    tok_ref,
    line,
    units,
    split,
    copy_sem,
    load_sem,
    cross_sem,
    swap_sem,
    lend_sem,
    lent_sem,
    part_sem,
    dsend_sem,
    drecv_sem,
    csend_sem,
    crecv_sem,
    fsend_sem,
    frecv_sem,
    *sems,
):
    dp = lax.axis_index("dp")
    ex = lax.axis_index("expert")
    plane, core = ex // 2, lax.rem(ex, 2)

    z, x = dp // XS, lax.rem(dp, XS)

    def peer(offset, its_core):
        return (dp, lax.rem(plane + offset + PLANES, PLANES) * 2 + its_core)

    partner = peer(0, 1 - core)
    opposite = peer(PLANES // 2, core)
    barrier = pltpu.get_barrier_semaphore()
    for offset in (1, -1, 2, -2):
        for half in range(2):
            pl.semaphore_signal(barrier, inc=1, device_id=peer(offset, half), device_id_type=MESH)
    for device in (partner, opposite):
        pl.semaphore_signal(barrier, inc=1, device_id=device, device_id_type=MESH)
    greet_dp(barrier, z, x, ex)

    load_tokens = pltpu.make_async_copy(tok_hbm, tok_ref, copy_sem.at[2])
    loads = [
        pltpu.make_async_copy(wg_ref, own.at[core, pl.ds(0, 16)], load_sem.at[0]),
        pltpu.make_async_copy(wu_ref, own.at[core, pl.ds(16, 16)], load_sem.at[1]),
    ] + [
        pltpu.make_async_copy(
            wd_ref.at[0, :, pl.ds(i * SQUARE, SQUARE)], own.at[core, 32 + i], load_sem.at[2 + i]
        )
        for i in range(16)
    ]
    for copy in loads:
        copy.start()
    load_tokens.start()

    route0 = mixed_ref[1:2, 0:TOK].astype(jnp.int32)
    route1 = mixed_ref[2:3, 0:TOK].astype(jnp.int32)
    scalars = mixed_ref[5:6, 0:TOK]
    experts = lax.broadcasted_iota(jnp.int32, (8, TOK), 0)
    named = ((route0 == experts) | (route1 == experts)).astype(F32)
    earlier = (
        lax.broadcasted_iota(jnp.int32, (TOK, TOK), 0) < lax.broadcasted_iota(jnp.int32, (TOK, TOK), 1)
    ).astype(BF16)
    slot = jnp.dot(named.astype(BF16), earlier, preferred_element_type=F32)
    row = lax.broadcasted_iota(jnp.int32, (PLANES * CAP, 1), 0)
    place = row // CAP
    offset_of = jnp.where(place % 2 == 1, (place + 1) // 2, (PLANES - place // 2) % PLANES)
    expert_of = (plane + offset_of) % PLANES
    spread = (expert_of == lax.broadcasted_iota(jnp.int32, (PLANES * CAP, 8), 1)).astype(BF16)
    slot_of = jnp.dot(spread, slot.astype(BF16), preferred_element_type=F32)
    fits = slot_of == (row % CAP).astype(F32)
    hot0 = (fits & (route0 == expert_of)).astype(F32)
    hot1 = (fits & (route1 == expert_of)).astype(F32)
    hot = (hot0 + hot1).astype(BF16)
    blend = (hot0 * mixed_ref[3:4, 0:TOK] + hot1 * mixed_ref[4:5, 0:TOK]).T
    blend_high = blend.astype(BF16)
    blend_low = (blend - blend_high.astype(F32)).astype(BF16)

    for copy in loads:
        copy.wait()
    pl.semaphore_wait(barrier, 10 + XS + 3)
    crosses = [
        pltpu.make_async_remote_copy(
            own.at[core, dp, rows],
            far.at[dp, rows],
            cross_sem.at[0, i],
            cross_sem.at[1, i],
            device_id=opposite,
            device_id_type=MESH,
        )
        for i, rows in enumerate((pl.ds(0, WEIGHT_CUT), pl.ds(WEIGHT_CUT, SQUARE - WEIGHT_CUT)))
    ]
    for copy in crosses:
        copy.start()
    load_tokens.wait()

    def to_partner(src, dst, send_sem, recv_sem):
        return pltpu.make_async_remote_copy(
            src, dst, send_sem, recv_sem, device_id=partner, device_id_type=MESH
        )

    def dispatch(p, half):
        return pltpu.make_async_remote_copy(
            sbuf.at[2 * p + half],
            rbuf.at[2 * TWIN[p] + core],
            dsend_sem.at[2 * p + half],
            drecv_sem.at[2 * TWIN[p] + core],
            device_id=peer(DY[p], half),
            device_id_type=MESH,
        )

    def give_back(q, half):
        return pltpu.make_async_remote_copy(
            obuf.at[2 * q + half],
            ret.at[2 * TWIN[q] + core],
            csend_sem.at[2 * q + half],
            crecv_sem.at[2 * TWIN[q] + core],
            device_id=peer(SOURCE[q], half),
            device_id_type=MESH,
        )

    def within(p, src, dst, send_sem, recv_sem):
        keep = pltpu.make_async_copy(src.at[2 * p + core], dst.at[2 * p + core], copy_sem.at[p // 7])
        give = to_partner(
            src.at[2 * p + 1 - core], dst.at[2 * p + core], send_sem.at[2 * p], recv_sem.at[2 * p]
        )
        return keep, give

    staying = [copy for p in (0, 7) for copy in within(p, sbuf, rbuf, dsend_sem, drecv_sem)]
    for p in PACK_ORDER:
        rows = jnp.dot(hot[p * CAP : (p + 1) * CAP], tok_ref[...], preferred_element_type=F32).astype(BF16)
        sbuf[2 * p : 2 * p + 2] = rows.reshape(2, HALF, D)
    for p in PACK_ORDER[:2]:
        for half in range(2):
            dispatch(p, half).start()
    for copy in staying:
        copy.start()
    swap = to_partner(own.at[core], own.at[core], swap_sem.at[0], swap_sem.at[1])
    swap.start()

    def arrived(ref, sem, i):
        pltpu.make_async_copy(ref.at[i], ref.at[i], sem.at[i]).wait()

    def activate(rows, gate_block, up_block):
        gate = jnp.dot(rows(), gate_block(), preferred_element_type=F32)
        up = jnp.dot(rows(), up_block(), preferred_element_type=F32)
        return (gate / (1.0 + jnp.exp(-gate)) * up).astype(BF16)

    def expand(low, high, h):
        return activate(
            lambda: rbuf[2 * low : 2 * high].reshape((high - low) * CAP, D),
            lambda: own[h, 0:16].reshape(D, FF),
            lambda: own[h, 16:32].reshape(D, FF),
        )

    def reduce(low, high, hidden):
        for t in range(16):
            cols = slice(t * SQUARE, (t + 1) * SQUARE)
            part0 = jnp.dot(hidden[0], own[0, 32 + t], preferred_element_type=F32).astype(BF16)
            part1 = jnp.dot(hidden[1], own[1, 32 + t], preferred_element_type=F32).astype(BF16)
            total = (part0.astype(F32) + part1.astype(F32)).astype(BF16)
            obuf[2 * low : 2 * high, :, cols] = total.reshape(2 * (high - low), HALF, SQUARE)
        for q in range(low, high):
            if q:
                for half in range(2):
                    give_back(q, half).start()

    lend = [
        to_partner(rbuf.at[10 + i], rbuf.at[16 + i], lend_sem.at[i], lent_sem.at[i]) for i in range(6)
    ]
    state = {}

    def between(step):
        if step == -1:
            for p in PACK_ORDER[2:6]:
                for half in range(2):
                    dispatch(p, half).start()
        elif step == 2:
            swap.wait()
            for i in range(6, 10):
                arrived(rbuf, drecv_sem, i)
            state["far"] = [expand(3, 5, h) for h in range(2)]
        elif step == 3:
            reduce(3, 5, state["far"])
            for copy in staying:
                copy.wait()
            for i in range(2, 6):
                arrived(rbuf, drecv_sem, i)
            state["near"] = [expand(0, 3, 0)]
        elif step == 4:
            state["near"].append(expand(0, 3, 1))
            reduce(0, 3, state["near"])
        elif step == 5:
            for i in range(10, 14):
                arrived(rbuf, drecv_sem, i)
            for copy in lend:
                copy.start()

    started = weight_gather(z, x, ex, far, crosses, sems[:7], between)
    for copy in lend:
        copy.wait()
    hidden = activate(
        lambda: rbuf[10:22].reshape(12 * HALF, D),
        lambda: far[0:16].reshape(D, FF),
        lambda: far[16:32].reshape(D, FF),
    )
    quarter = D // 4
    parts = []
    for t in range(4):
        for i in range(4):
            cols = slice(t * quarter + i * SQUARE, t * quarter + (i + 1) * SQUARE)
            part = jnp.dot(hidden, far[32 + 4 * t + i], preferred_element_type=F32).astype(BF16)
            obuf[10:16, :, cols] = part[: 6 * HALF].reshape(6, HALF, SQUARE)
            theirs[:, :, cols] = part[6 * HALF :].reshape(6, HALF, SQUARE)
        whole = pl.ds(t * quarter, quarter)
        parts.append(
            to_partner(theirs.at[:, :, whole], got.at[:, :, whole], part_sem.at[0, t], part_sem.at[1, t])
        )
        parts[t].start()
    returning = []
    for t in range(4):
        parts[t].wait()
        cols = slice(t * quarter, (t + 1) * quarter)
        whole = pl.ds(t * quarter, quarter)
        for i in (0, 2, 4):
            total = obuf[10 + i : 12 + i, :, cols].astype(F32) + got[i : i + 2, :, cols].astype(F32)
            obuf[10 + i : 12 + i, :, cols] = total.astype(BF16)
            if i < 4:
                for half in range(2):
                    q = 5 + i // 2
                    returning.append(
                        pltpu.make_async_remote_copy(
                            obuf.at[2 * q + half, :, whole],
                            ret.at[2 * q + core, :, whole],
                            fsend_sem.at[t, i + half],
                            frecv_sem.at[t, i + core],
                            device_id=peer(SOURCE[q], half),
                            device_id_type=MESH,
                        )
                    )
                    returning[-1].start()
    final = [copy for q in (0, 7) for copy in within(q, obuf, ret, csend_sem, crecv_sem)]
    for copy in final:
        copy.start()

    for copy in started:
        copy.wait_send()
    for p in range(1, 7):
        for half in range(2):
            dispatch(p, half).wait_send()
            if p < 5:
                give_back(p, half).wait_send()
    for copy in final:
        copy.wait()
    for i in range(2, 10):
        arrived(ret, crecv_sem, i)
    for copy in returning:
        copy.wait_send()
    for t in range(4):
        whole = pl.ds(t * quarter, quarter)
        for i in range(4):
            pltpu.make_async_copy(
                ret.at[10 + i, :, whole], ret.at[10 + i, :, whole], frecv_sem.at[t, i]
            ).wait()

    squares = jnp.zeros((TOK, 1), F32)
    for t in range(8):
        cols = slice(t * 512, (t + 1) * 512)
        outs = ret[:, :, cols].reshape(PLANES * CAP, 512)
        mixed = jnp.dot(blend_high, outs, preferred_element_type=F32) + jnp.dot(
            blend_low, outs, preferred_element_type=F32
        )
        block = (tok_ref[:, cols].astype(F32) + mixed).astype(BF16)
        layer_ref[:, cols] = block
        lifted = block.astype(F32)
        squares += jnp.sum(lifted * lifted, axis=1, keepdims=True)
    scale = lax.rsqrt(squares / D + 1e-05)
    position = lax.broadcasted_iota(jnp.int32, (TOK, 1), 0).astype(F32)
    q_len, p_len = scalars[:, 0:1], scalars[:, 1:2]
    q_coef = jnp.where(position < q_len, scale, 0.0) / q_len
    p_coef = jnp.where((position >= QLEN) & (position < QLEN + p_len), scale, 0.0) / p_len
    q_sum = jnp.zeros((1, 1), F32)
    p_sum = jnp.zeros((1, 1), F32)
    for t in range(8):
        cols = slice(t * 512, (t + 1) * 512)
        lifted = layer_ref[:, cols].astype(F32)
        gain = mixed_ref[0:1, cols]
        q_vec = jnp.sum(lifted[:QLEN] * q_coef[:QLEN], axis=0, keepdims=True) * gain
        p_vec = jnp.sum(lifted[QLEN:] * p_coef[QLEN:], axis=0, keepdims=True) * gain
        q_sum += jnp.sum(q_vec * q_vec, axis=1, keepdims=True)
        p_sum += jnp.sum(p_vec * p_vec, axis=1, keepdims=True)
        line[dp, 0:1, cols] = q_vec
        line[dp, 1:2, cols] = p_vec
    kind = lax.broadcasted_iota(jnp.int32, (2, 1), 0)
    line[dp, :, 0:D] = line[dp, :, 0:D] * lax.rsqrt(jnp.where(kind == 0, q_sum, p_sum) + 1e-06)
    lane = lax.broadcasted_iota(jnp.int32, (2, META), 1)
    line[dp, :, D:WIDE] = jnp.where(
        lane == 0, scalars[:, 3:4], jnp.where(lane == 1, scalars[:, 2:3], 0.0)
    )
    started = line_gather(z, x, ex, line, sems[7:])

    def merge(group, carry):
        for i in range(XS):
            units[group, 2 * i : 2 * i + 2, :] = line[XS * group + i]
        return carry

    lax.fori_loop(0, ZS, merge, 0)

    def divide(group, carry):
        rows = units[pl.ds(2 * group, 2), :, 0:D].reshape(16, D)
        high = rows.astype(BF16)
        split[0, group] = high
        split[1, group] = (rows - high.astype(F32)).astype(BF16)
        return carry

    lax.fori_loop(0, ZS // 2, divide, 0)
    for copy in started:
        copy.wait_send()

    meta = units[:, :, D:WIDE].reshape(RANKS, META)
    sharp, positive = meta[:, 0:1], meta[:, 1:2]
    across = (((1,), (1,)), ((), ()))
    high_gram = lax.dot_general(
        split[...].reshape(2 * RANKS, D), split[0].reshape(RANKS, D), across, preferred_element_type=F32
    )
    low_gram = lax.dot_general(
        split[0].reshape(RANKS, D), split[1].reshape(RANKS, D), across, preferred_element_type=F32
    )
    gram = high_gram[:RANKS] + (high_gram[RANKS:] + low_gram)
    row = lax.broadcasted_iota(jnp.int32, (RANKS, RANKS), 0)
    col = lax.broadcasted_iota(jnp.int32, (RANKS, RANKS), 1)
    is_passage = col % 2 == 1
    scores = jnp.where(is_passage, gram * sharp, -jnp.inf)
    expos = jnp.exp(scores - jnp.max(scores, axis=1, keepdims=True))
    probs = expos / jnp.sum(expos, axis=1, keepdims=True)
    target = (is_passage & ((col // 2).astype(F32) == positive)).astype(F32)
    coef = jnp.where((row % 2 == 0) & is_passage, (probs - target) * sharp / (RANKS // 2), 0.0)
    pick_row = lax.broadcasted_iota(jnp.int32, (8, RANKS), 0)
    pick_col = lax.broadcasted_iota(jnp.int32, (8, RANKS), 1)
    own_query = ((pick_row == 0) & (pick_col == 2 * dp)).astype(F32)
    own_passage = ((pick_row == 1) & (pick_col == 2 * dp + 1)).astype(F32)
    picked = jnp.dot(own_query, coef, precision=HIGHEST, preferred_element_type=F32) + lax.dot_general(
        own_passage, coef, (((1,), (1,)), ((), ())), precision=HIGHEST, preferred_element_type=F32
    )
    picked_high = picked.astype(BF16)
    picked_low = (picked - picked_high.astype(F32)).astype(BF16)
    both = jnp.concatenate([picked_high.astype(F32), picked_low.astype(F32)], axis=0).astype(BF16)
    for t in range(4):
        cols = slice(t * 1024, (t + 1) * 1024)
        top = jnp.dot(both, split[0, :, :, cols].reshape(RANKS, 1024), preferred_element_type=F32)
        low = jnp.dot(both, split[1, :, :, cols].reshape(RANKS, 1024), preferred_element_type=F32)
        grads_ref[0, :, cols] = top[0:2] + (top[8:10] + low[0:2])


def vmem(shape, dtype):
    return pltpu.VMEM(shape, dtype)


def local(
    tokens, routes, route_weights, w_gate, w_up, w_down, rms_gain, query_len, passage_len, positive, logit_scale
):
    in_vmem = pl.BlockSpec(memory_space=pltpu.VMEM)
    anywhere = pl.BlockSpec(memory_space=pl.ANY)
    dma = pltpu.SemaphoreType.DMA
    slots = 2 * PLANES
    places = [(0, 0, rms_gain[None]), (1, 0, routes.T.astype(F32)), (3, 0, route_weights.T)]
    for i, v in enumerate((query_len, passage_len, positive, logit_scale)):
        places.append((5, i, v.reshape(1, 1).astype(F32)))
    mixed = 0.0
    for row, column, v in places:
        mixed += jnp.pad(v, ((row, 8 - row - v.shape[0]), (column, D - column - v.shape[1])))
    return pl.pallas_call(
        moe_kernel,
        out_shape=(
            jax.ShapeDtypeStruct((TOK, D), BF16),
            jax.ShapeDtypeStruct((1, 2, D), F32),
        ),
        in_specs=[anywhere, in_vmem] + [anywhere] * 3,
        out_specs=(in_vmem, in_vmem),
        scratch_shapes=[
            vmem((slots, HALF, D), BF16),
            vmem((slots + 6, HALF, D), BF16),
            vmem((slots, HALF, D), BF16),
            vmem((slots, HALF, D), BF16),
            vmem((2, BLOCKS, SQUARE, SQUARE), BF16),
            vmem((BLOCKS, SQUARE, SQUARE), BF16),
            vmem((6, HALF, D), BF16),
            vmem((6, HALF, D), BF16),
            vmem((TOK, D), BF16),
            vmem((BLOCKS, 2, WIDE), F32),
            vmem((ZS, 8, WIDE), F32),
            vmem((2, ZS // 2, 16, D), BF16),
            dma((3,)),
            dma((18,)),
            dma((2, 2)),
            dma((2,)),
            dma((6,)),
            dma((6,)),
            dma((2, 4)),
            dma((slots,)),
            dma((slots,)),
            dma((slots,)),
            dma((slots,)),
            dma((4, 4)),
            dma((4, 4)),
        ]
        + weight_sems()
        + line_sems(),
        compiler_params=pltpu.CompilerParams(
            collective_id=0, has_side_effects=True, vmem_limit_bytes=52 * 2**20
        ),
        name="moe",
    )(
        tokens,
        mixed,
        w_gate.reshape(16, SQUARE, FF),
        w_up.reshape(16, SQUARE, FF),
        w_down,
    )


def solution(mesh):
    return jax.shard_map(
        local,
        mesh=mesh,
        in_specs=(
            P(("dp", "expert"), None),
            P(("dp", "expert"), None),
            P(("dp", "expert"), None),
            P("expert", None, None),
            P("expert", None, None),
            P("expert", None, None),
            P(),
            P(("dp", "expert")),
            P(("dp", "expert")),
            P("expert", "dp"),
            P("expert", "dp"),
        ),
        out_specs=(P(("dp", "expert"), None), P(("dp", "expert"), None, None)),
        check_vma=False,
    )
```
